256 devices in a mesh: tok: 16 (over y, x), code: 16 (over z, core).
Axes of the slice: x: 4, y: 4, z: 8, core: 2. Of those that a mesh axis runs over, the one named last changes fastest.
Arguments:
- tokens: bfloat16 [4096, 512], P('tok'), may hold values from -128 to 128
- codebook: bfloat16 [65536, 512], P('code'), may hold values from -1 to 1
Outputs:
- targets: bfloat16 [4096, 65536], P('tok', 'code')
- updated_codebook: float32 [65536, 512], P(('code', 'tok'))
The draws below stay inside these ranges and needn't reach their ends.
All inputs are finite; a program needn't handle non-finite values.
Results may differ from the reference program's by a relative error of at most 0.011.
Values may be sent and summed in bfloat16 or wider, within the bound.
No kernel may reach another device: no remote copies, remote signals or barrier semaphores. Data moves between devices by JAX's collectives and lax.ppermute only.
A program may use at most 64 MiB of HBM per device.

```python
import math
import jax
import jax.numpy as jnp
from jax import lax

D = 512
CODE_DEV = 4096
ITERS = 3
CODES = 65536
TOKEN_TOTAL = 4096


def shared_codes(key):
    inner = jax.random.fold_in(key, 11)
    entries = jax.random.normal(inner, (CODES, D), jnp.float32)
    return jnp.clip(entries, -4.0, 4.0) * D ** (-0.5)


def draw_codebook(key, part):
    entries = shared_codes(key)
    return entries.astype(jnp.bfloat16)


def draw_tokens(key, part):
    key = jax.random.fold_in(key, 7)
    keys = jax.random.split(key, 2)
    scales = jnp.exp(jax.random.uniform(keys[0], (TOKEN_TOTAL, 1), jnp.float32, jnp.log(0.5), jnp.log(5.0)))
    values = jnp.clip(jax.random.normal(keys[1], (TOKEN_TOTAL, D), jnp.float32), -6.0, 6.0) * scales
    values = jnp.clip(values, -128.0, 128.0)
    return values.astype(jnp.bfloat16)


def setup_inputs(seed: int = 0) -> dict:
    seeds = jax.random.split(jax.random.key(seed), 3)
    tokens = draw_tokens(jax.random.fold_in(seeds[2], 71), 0)
    codebook = draw_codebook(jax.random.fold_in(seeds[2], 71), 0)
    return dict(tokens=tokens, codebook=codebook)


sharpness_factor = 2.5
rms_epsilon = 1e-06

def reference(tokens, codebook):
    blocks = CODES // CODE_DEV
    code_blocks = codebook.reshape(blocks, CODE_DEV, D)

    def block_score_matrix(token_block):
        return jnp.dot(tokens, token_block.T, preferred_element_type=jnp.float32) * sharpness_factor
    scores = lax.map(block_score_matrix, code_blocks)
    token_potential = jnp.zeros((TOKEN_TOTAL,), jnp.float32)

    def column_potential(tile):
        return -math.log(CODES) - jax.nn.logsumexp(tile + token_potential[:, None], axis=0)
    for step in range(ITERS):
        code_potential = lax.map(column_potential, scores)

        def row_stride(carry, inputs):
            tile, potential = inputs
            values = tile + potential[None, :]
            local = lax.optimization_barrier(jnp.max(values, axis=1))
            top = jnp.maximum(carry[0], local)
            total = carry[1] * jnp.exp(carry[0] - top) + lax.optimization_barrier(jnp.sum(jnp.exp(values - top[:, None]), axis=1))
            return ((top, total), None)
        start = (jnp.full((TOKEN_TOTAL,), -jnp.inf, jnp.float32), jnp.zeros((TOKEN_TOTAL,), jnp.float32))
        (top, total), unused = lax.scan(row_stride, start, (scores, code_potential))
        token_potential = -math.log(TOKEN_TOTAL) - (top + jnp.log(total))

    def finish(inputs):
        tile, potential, token_block = inputs
        weights = (TOKEN_TOTAL * jnp.exp(tile + token_potential[:, None] + potential[None, :])).astype(jnp.bfloat16)
        assigned = jnp.dot(weights.T, tokens, preferred_element_type=jnp.float32)
        mixed = token_block.astype(jnp.float32) + assigned
        refreshed = mixed * lax.rsqrt(lax.optimization_barrier(jnp.mean(mixed * mixed, axis=1, keepdims=True)) + rms_epsilon)
        return (weights, refreshed)
    weights, refreshed = lax.map(finish, (scores, code_potential, code_blocks))
    targets = jnp.moveaxis(weights, 0, 1).reshape(TOKEN_TOTAL, CODES)
    return (targets, refreshed.reshape(CODES, D))
```

```python
import functools
import math

import jax
import jax.numpy as jnp
from jax import lax
from jax.experimental import pallas as pl
from jax.experimental.pallas import tpu as pltpu
from jax.sharding import PartitionSpec as P

ITERS = 3


sharpness_factor = 2.5
rms_epsilon = 1e-06

LANES = 128
CHUNK = 512
MIB = 1 << 20

score_scale = sharpness_factor * math.log2(math.e)


def lse2(values, axis):
    top = jnp.max(values, axis=axis, keepdims=True)
    total = jnp.sum(jnp.exp2(values - top), axis=axis)
    return jnp.squeeze(top, axis) + jnp.log2(total)


def as_column(row):
    return jnp.broadcast_to(row, (LANES, LANES)).T


def tile(k):
    return pl.ds(pl.multiple_of(k * LANES, LANES), LANES)


def column_lse(scores, potential, k):
    values = scores[:, tile(k)]
    if potential is not None:
        values = values + potential[...]
    values = values.reshape(values.shape[0] // 8, 8, LANES)
    top = jnp.max(values, axis=0)
    total = jnp.sum(jnp.exp2(values - top[None]), axis=0)
    most = jnp.max(top, axis=0, keepdims=True)
    total = jnp.sum(total * jnp.exp2(top - most), axis=0, keepdims=True)
    return most + jnp.log2(total)


def send_copies(local, out):
    for d in range(out.shape[0]):
        out[d] = local[...]


def scores_kernel(tokens, codebook, scores, out, held, local, sems):
    chunks = codebook.shape[0] // CHUNK
    copies = [
        pltpu.make_async_copy(
            codebook.at[pl.ds(k * CHUNK, CHUNK)], held.at[pl.ds(k * CHUNK, CHUNK)], sems.at[k]
        )
        for k in range(chunks)
    ]
    for copy in copies:
        copy.start()
    for k in range(chunks):
        copies[k].wait()
        scores[:, pl.ds(k * CHUNK, CHUNK)] = (
            lax.dot_general(
                tokens[...],
                held[pl.ds(k * CHUNK, CHUNK), :],
                (((1,), (1,)), ((), ())),
                preferred_element_type=jnp.float32,
            )
            * score_scale
        )
        for j in range(k * CHUNK // LANES, (k + 1) * CHUNK // LANES):
            local[pl.ds(j, 1), :] = column_lse(scores, None, j)
    send_copies(local, out)


def columns_kernel(shift, received, scores, out, column, local):
    potential = -shift - lse2(received[...], 0)
    for h in range(potential.shape[0]):
        column[pl.ds(h * LANES, LANES), :] = as_column(potential[h : h + 1, :])

    def step(k, carry):
        local[pl.ds(k, 1), :] = column_lse(scores, column, k)
        return carry

    lax.fori_loop(0, local.shape[0], step, 0, unroll=4)
    send_copies(local, out)


def rows_kernel(shift, received, scores, out, potential, local):
    potential[...] = -shift - lse2(received[...], 0)
    tiles = potential.shape[0]
    for h in range(local.shape[0]):
        rows = pl.ds(h * LANES, LANES)

        def values(k):
            return scores[rows, tile(k)] + potential[pl.ds(k, 1), :]

        top = lax.fori_loop(
            0, tiles, lambda k, top: jnp.maximum(top, values(k)), values(0), unroll=4
        )
        total = lax.fori_loop(
            0,
            tiles,
            lambda k, total: total + jnp.exp2(values(k) - top),
            jnp.zeros((LANES, LANES), jnp.float32),
            unroll=4,
        )
        top = top.T
        most = jnp.max(top, axis=0, keepdims=True)
        total = jnp.sum(total.T * jnp.exp2(top - most), axis=0, keepdims=True)
        local[pl.ds(h, 1), :] = most + jnp.log2(total)
    send_copies(local, out)


def token_potential_kernel(shift, received, out):
    potential = -shift - lse2(received[...], 0)
    for d in range(out.shape[0]):
        out[d] = potential


def targets_kernel(scale, token_potential, code_potential, scores, out, column, held, sems):
    for h in range(token_potential.shape[0]):
        column[pl.ds(h * LANES, LANES), :] = as_column(token_potential[h : h + 1, :]) + scale
    copies = []
    for k in range(scores.shape[1] // CHUNK):
        for j in range(k * CHUNK // LANES, (k + 1) * CHUNK // LANES):
            held[:, tile(j)] = jnp.exp2(
                scores[:, tile(j)] + column[...] + code_potential[pl.ds(j, 1), :]
            ).astype(held.dtype)
        part = (slice(None), pl.ds(k * CHUNK, CHUNK))
        copies.append(pltpu.make_async_copy(held.at[part], out.at[part], sems.at[k]))
        copies[k].start()
    for copy in copies:
        copy.wait()


def own_scores_kernel(scale, codes, potential, tokens, scores, held, column, sems):
    chunks = tokens.shape[0] // CHUNK
    copies = [
        pltpu.make_async_copy(
            tokens.at[pl.ds(k * CHUNK, CHUNK)], held.at[pl.ds(k * CHUNK, CHUNK)], sems.at[k]
        )
        for k in range(chunks)
    ]
    for copy in copies:
        copy.start()
    for h in range(potential.shape[0]):
        column[pl.ds(h * LANES, LANES), :] = as_column(potential[h : h + 1, :]) + scale
    for k in range(chunks):
        copies[k].wait()
        values = lax.dot_general(
            codes[...],
            held[pl.ds(k * CHUNK, CHUNK), :],
            (((1,), (1,)), ((), ())),
            preferred_element_type=jnp.float32,
        )
        for j in range(CHUNK // LANES):
            scores[:, pl.ds(k * CHUNK + j * LANES, LANES)] = (
                values[:, j * LANES : (j + 1) * LANES] * score_scale + column[...]
            )


def refresh_kernel(codes, potential, scores, tokens, out):
    halves = potential.shape[1]
    assigned = jnp.zeros(out.shape, jnp.float32)
    for k in range(tokens.shape[0] // CHUNK):
        parts = []
        for j in range(k * CHUNK // LANES, (k + 1) * CHUNK // LANES):
            row = potential[j // halves, pl.ds(j % halves, 1), :]
            parts.append(jnp.exp2(scores[:, tile(j)] + row).astype(tokens.dtype))
        assigned += jnp.dot(
            jnp.concatenate(parts, axis=1),
            tokens[pl.ds(k * CHUNK, CHUNK), :],
            preferred_element_type=jnp.float32,
        )
    mixed = codes[...].astype(jnp.float32) + assigned
    out[...] = mixed * lax.rsqrt(
        jnp.mean(mixed * mixed, axis=1, keepdims=True) + rms_epsilon
    )


def in_vmem(array):
    return pltpu.with_memory_space_constraint(array, pltpu.VMEM)


def call(kernel, out_shape, scratch=(), specs=None, out_specs=None, limit=24, elements=0, flops=0):
    vmem = pl.BlockSpec(memory_space=pltpu.VMEM)
    return pl.pallas_call(
        kernel,
        out_shape=out_shape,
        in_specs=specs,
        out_specs=out_specs if out_specs is not None else jax.tree.map(lambda _: vmem, out_shape),
        scratch_shapes=list(scratch),
        compiler_params=pltpu.CompilerParams(vmem_limit_bytes=limit * MIB),
        cost_estimate=pl.CostEstimate(
            flops=flops + 4 * elements, transcendentals=elements, bytes_accessed=4 * elements
        ),
    )


def per_device(tokens, codebook):
    tok_size, code_size = lax.axis_size("tok"), lax.axis_size("code")
    tok_rows, depth = tokens.shape
    code_rows = codebook.shape[0]
    total_tokens = tok_rows * tok_size
    total_codes = code_rows * code_size
    share = code_rows // tok_size
    row_tiles, code_tiles = tok_rows // LANES, code_rows // LANES
    elements = tok_rows * code_rows
    f32 = jnp.float32
    vmem = pl.BlockSpec(memory_space=pltpu.VMEM)
    hbm = pl.BlockSpec(memory_space=pl.ANY)
    resident = functools.partial(pltpu.VMEM, dtype=f32)
    to_tok = jax.ShapeDtypeStruct((tok_size, code_tiles, LANES), f32)
    to_code = jax.ShapeDtypeStruct((code_size, row_tiles, LANES), f32)
    column = pltpu.VMEM((tok_rows, LANES), f32)

    def exchange(copies, axis):
        return lax.all_to_all(copies, axis, 0, 0)

    all_tokens = lax.all_gather(tokens, "tok", axis=0, tiled=True)

    scores, copies = call(
        scores_kernel,
        (pltpu.VMEM((tok_rows, code_rows), f32), to_tok),
        [
            pltpu.VMEM((code_rows, depth), codebook.dtype),
            pltpu.VMEM((code_tiles, LANES), f32),
            pltpu.SemaphoreType.DMA((code_rows // CHUNK,)),
        ],
        specs=[vmem, hbm],
        elements=elements,
        flops=2 * elements * depth,
    )(tokens, codebook)
    for step in range(ITERS):
        received = exchange(copies, "tok")
        copies, code_potential = call(
            functools.partial(rows_kernel, math.log2(total_codes)),
            (to_code, jax.ShapeDtypeStruct((code_tiles, LANES), f32)),
            [pltpu.VMEM((row_tiles, LANES), f32)],
            specs=[vmem, vmem],
            elements=elements,
        )(received, in_vmem(scores))
        received = exchange(copies, "code")
        if step < ITERS - 1:
            copies = call(
                functools.partial(columns_kernel, math.log2(total_tokens)),
                to_tok,
                [column, pltpu.VMEM((code_tiles, LANES), f32)],
                specs=[vmem, vmem],
                elements=elements,
            )(received, in_vmem(scores))

    place = lax.axis_index("tok")
    own_codes = lax.dynamic_slice_in_dim(codebook, place * share, share, 0)
    share_tiles = share // LANES
    own_potential = lax.dynamic_slice_in_dim(code_potential, place * share_tiles, share_tiles, 0)
    own_scores, held_tokens = call(
        functools.partial(own_scores_kernel, math.log2(total_tokens)),
        (
            pltpu.VMEM((share, total_tokens), f32),
            pltpu.VMEM((total_tokens, depth), tokens.dtype),
        ),
        [
            pltpu.VMEM((share, LANES), f32),
            pltpu.SemaphoreType.DMA((total_tokens // CHUNK,)),
        ],
        specs=[vmem, vmem, hbm],
        elements=elements,
        flops=2 * elements * depth,
    )(own_codes, own_potential, all_tokens)

    copies = call(
        functools.partial(token_potential_kernel, math.log2(total_tokens)),
        jax.ShapeDtypeStruct((tok_size, row_tiles, LANES), f32),
        specs=[vmem],
    )(received)
    all_potential = exchange(copies, "tok")
    targets = call(
        functools.partial(targets_kernel, math.log2(total_tokens)),
        jax.ShapeDtypeStruct((tok_rows, code_rows), jnp.bfloat16),
        [
            column,
            pltpu.VMEM((tok_rows, code_rows), jnp.bfloat16),
            pltpu.SemaphoreType.DMA((code_rows // CHUNK,)),
        ],
        specs=[vmem, vmem, vmem],
        out_specs=hbm,
        elements=elements,
    )(copies[0], code_potential, in_vmem(scores))
    updated_codebook = call(
        refresh_kernel,
        jax.ShapeDtypeStruct((share, depth), f32),
        specs=[vmem, vmem, vmem, vmem],
        elements=elements,
        flops=2 * elements * depth,
    )(own_codes, all_potential, in_vmem(own_scores), in_vmem(held_tokens))
    return (targets, updated_codebook)


def solution(mesh):
    return jax.shard_map(
        per_device,
        mesh=mesh,
        in_specs=(P("tok", None), P("code", None)),
        out_specs=(P("tok", "code"), P(("code", "tok"), None)),
        check_vma=False,
    )
```

```python
import functools
import math

import jax
import jax.numpy as jnp
from jax import lax
from jax.experimental import pallas as pl
from jax.experimental.pallas import tpu as pltpu
from jax.sharding import PartitionSpec as P

ITERS = 3


sharpness_factor = 2.5
rms_epsilon = 1e-06

LANES = 128
CHUNK = 512
MIB = 1 << 20

score_scale = sharpness_factor * math.log2(math.e)


def lse2(values, axis):
    top = jnp.max(values, axis=axis, keepdims=True)
    total = jnp.sum(jnp.exp2(values - top), axis=axis)
    return jnp.squeeze(top, axis) + jnp.log2(total)


def as_column(row):
    return jnp.broadcast_to(row, (LANES, LANES)).T


def tile(k):
    return pl.ds(pl.multiple_of(k * LANES, LANES), LANES)


def column_lse(scores, potential, k):
    values = scores[:, tile(k)]
    if potential is not None:
        values = values + potential[...]
    values = values.reshape(values.shape[0] // 8, 8, LANES)
    top = jnp.max(values, axis=0)
    total = jnp.sum(jnp.exp2(values - top[None]), axis=0)
    most = jnp.max(top, axis=0, keepdims=True)
    total = jnp.sum(total * jnp.exp2(top - most), axis=0, keepdims=True)
    return most + jnp.log2(total)


def send_copies(local, out):
    for d in range(out.shape[0]):
        out[d] = local[...]


def chunk_copies(source, held, sems, axis=0):
    copies = []
    for k in range(source.shape[axis] // CHUNK):
        part = (slice(None),) * axis + (pl.ds(k * CHUNK, CHUNK),)
        copies.append(pltpu.make_async_copy(source.at[part], held.at[part], sems.at[k]))
    return copies


def scores_kernel(tokens, codebook, scores, out, held, local, sems):
    copies = chunk_copies(codebook, held, sems)
    for copy in copies:
        copy.start()
    for k in range(len(copies)):
        copies[k].wait()
        scores[:, pl.ds(k * CHUNK, CHUNK)] = (
            lax.dot_general(
                tokens[...],
                held[pl.ds(k * CHUNK, CHUNK), :],
                (((1,), (1,)), ((), ())),
                preferred_element_type=jnp.float32,
            )
            * score_scale
        )
        for j in range(k * CHUNK // LANES, (k + 1) * CHUNK // LANES):
            local[pl.ds(j, 1), :] = column_lse(scores, None, j)
    send_copies(local, out)


def columns_kernel(shift, received, scores, out, column, local):
    potential = -shift - lse2(received[...], 0)
    for h in range(potential.shape[0]):
        column[pl.ds(h * LANES, LANES), :] = as_column(potential[h : h + 1, :])

    def step(k, carry):
        local[pl.ds(k, 1), :] = column_lse(scores, column, k)
        return carry

    lax.fori_loop(0, local.shape[0], step, 0, unroll=4)
    send_copies(local, out)


def rows_kernel(shift, received, scores, out, potential, local):
    potential[...] = -shift - lse2(received[...], 0)
    tiles = potential.shape[0]
    for h in range(local.shape[0]):
        rows = pl.ds(h * LANES, LANES)

        def values(k):
            return scores[rows, tile(k)] + potential[pl.ds(k, 1), :]

        top = lax.fori_loop(
            0, tiles, lambda k, top: jnp.maximum(top, values(k)), values(0), unroll=4
        )
        total = lax.fori_loop(
            0,
            tiles,
            lambda k, total: total + jnp.exp2(values(k) - top),
            jnp.zeros((LANES, LANES), jnp.float32),
            unroll=4,
        )
        top = top.T
        most = jnp.max(top, axis=0, keepdims=True)
        total = jnp.sum(total.T * jnp.exp2(top - most), axis=0, keepdims=True)
        local[pl.ds(h, 1), :] = most + jnp.log2(total)
    send_copies(local, out)


def token_potential_kernel(shift, received, out):
    potential = -shift - lse2(received[...], 0)
    for d in range(out.shape[0]):
        out[d] = potential


def targets_kernel(
    scale, token_potential, code_potential, scores, out, column, panel, held, sems, out_sems
):
    copies = chunk_copies(scores, panel, sems, 1)
    for copy in copies:
        copy.start()
    for h in range(token_potential.shape[1]):
        column[pl.ds(h * LANES, LANES), :] = as_column(token_potential[0, pl.ds(h, 1), :]) + scale
    out_copies = chunk_copies(held, out, out_sems, 1)
    for k in range(len(copies)):
        copies[k].wait()
        for j in range(k * CHUNK // LANES, (k + 1) * CHUNK // LANES):
            held[:, tile(j)] = jnp.exp2(
                panel[:, tile(j)] + column[...] + code_potential[pl.ds(j, 1), :]
            ).astype(held.dtype)
        out_copies[k].start()
    for copy in out_copies:
        copy.wait()


def refresh_kernel(
    scale, code_potential, potential, codebook, tokens, out, held, codes, column, sems, own_sem
):
    copies = chunk_copies(tokens, held, sems)
    share, halves = codes.shape[0], potential.shape[1]
    place = lax.axis_index("tok")
    own_rows = pl.ds(pl.multiple_of(place * share, share), share)
    own = pltpu.make_async_copy(codebook.at[own_rows], codes, own_sem)
    own.start()
    for copy in copies:
        copy.start()
    for h in range(share // LANES):
        row = code_potential[pl.ds(place * (share // LANES) + h, 1), :]
        column[pl.ds(h * LANES, LANES), :] = as_column(row) + scale
    own.wait()
    assigned = jnp.zeros(out.shape, jnp.float32)
    for k in range(len(copies)):
        copies[k].wait()
        part = held[pl.ds(k * CHUNK, CHUNK), :]
        scores = (
            lax.dot_general(
                codes[...], part, (((1,), (1,)), ((), ())), preferred_element_type=jnp.float32
            )
            * score_scale
        )
        weights = []
        for j in range(CHUNK // LANES):
            at = k * CHUNK // LANES + j
            row = potential[at // halves, pl.ds(at % halves, 1), :]
            values = scores[:, j * LANES : (j + 1) * LANES] + column[...] + row
            weights.append(jnp.exp2(values).astype(part.dtype))
        assigned += jnp.dot(
            jnp.concatenate(weights, axis=1), part, preferred_element_type=jnp.float32
        )
    mixed = codes[...].astype(jnp.float32) + assigned
    out[...] = mixed * lax.rsqrt(
        jnp.mean(mixed * mixed, axis=1, keepdims=True) + rms_epsilon
    )


def in_vmem(array):
    return pltpu.with_memory_space_constraint(array, pltpu.VMEM)


def in_hbm(array):
    return pltpu.with_memory_space_constraint(array, pltpu.HBM)


def call(kernel, out_shape, scratch=(), specs=None, out_specs=None, limit=24, elements=0, flops=0):
    vmem = pl.BlockSpec(memory_space=pltpu.VMEM)
    return pl.pallas_call(
        kernel,
        out_shape=out_shape,
        in_specs=specs,
        out_specs=out_specs if out_specs is not None else jax.tree.map(lambda _: vmem, out_shape),
        scratch_shapes=list(scratch),
        compiler_params=pltpu.CompilerParams(vmem_limit_bytes=limit * MIB),
        cost_estimate=pl.CostEstimate(
            flops=flops + 4 * elements, transcendentals=elements, bytes_accessed=4 * elements
        ),
    )


def per_device(tokens, codebook):
    tok_size, code_size = lax.axis_size("tok"), lax.axis_size("code")
    tok_rows, depth = tokens.shape
    code_rows = codebook.shape[0]
    total_tokens = tok_rows * tok_size
    total_codes = code_rows * code_size
    share = code_rows // tok_size
    row_tiles, code_tiles = tok_rows // LANES, code_rows // LANES
    elements = tok_rows * code_rows
    f32 = jnp.float32
    vmem = pl.BlockSpec(memory_space=pltpu.VMEM)
    hbm = pl.BlockSpec(memory_space=pltpu.HBM)
    resident = functools.partial(pltpu.VMEM, dtype=f32)
    to_tok = jax.ShapeDtypeStruct((tok_size, code_tiles, LANES), f32)
    to_code = jax.ShapeDtypeStruct((code_size, row_tiles, LANES), f32)
    column = pltpu.VMEM((tok_rows, LANES), f32)

    def exchange(copies, axis):
        return lax.all_to_all(copies, axis, 0, 0)

    all_tokens = lax.all_gather(tokens, "tok", axis=0, tiled=True)

    scores, copies = call(
        scores_kernel,
        (pltpu.VMEM((tok_rows, code_rows), f32), to_tok),
        [
            pltpu.VMEM((code_rows, depth), codebook.dtype),
            pltpu.VMEM((code_tiles, LANES), f32),
            pltpu.SemaphoreType.DMA((code_rows // CHUNK,)),
        ],
        specs=[vmem, hbm],
        elements=elements,
        flops=2 * elements * depth,
    )(tokens, in_hbm(codebook))
    for step in range(ITERS):
        last = step == ITERS - 1
        received = exchange(copies, "tok")
        potential = pltpu.VMEM((code_tiles, LANES), f32)
        row_partials = pltpu.VMEM((row_tiles, LANES), f32)
        copies, *code_potential = call(
            functools.partial(rows_kernel, math.log2(total_codes)),
            (to_code, potential) if last else (to_code,),
            [row_partials] if last else [potential, row_partials],
            specs=[vmem, vmem],
            elements=elements,
        )(received, in_vmem(scores))
        received = exchange(copies, "code")
        if not last:
            copies = call(
                functools.partial(columns_kernel, math.log2(total_tokens)),
                to_tok,
                [column, pltpu.VMEM((code_tiles, LANES), f32)],
                specs=[vmem, vmem],
                elements=elements,
            )(received, in_vmem(scores))
    (code_potential,) = code_potential

    copies = call(
        functools.partial(token_potential_kernel, math.log2(total_tokens)),
        jax.ShapeDtypeStruct((tok_size, row_tiles, LANES), f32),
        specs=[vmem],
    )(received)
    all_potential = exchange(copies, "tok")
    code_sems = pltpu.SemaphoreType.DMA((code_rows // CHUNK,))
    targets = call(
        functools.partial(targets_kernel, math.log2(total_tokens)),
        jax.ShapeDtypeStruct((tok_rows, code_rows), jnp.bfloat16),
        [
            column,
            pltpu.VMEM((tok_rows, code_rows), f32),
            pltpu.VMEM((tok_rows, code_rows), jnp.bfloat16),
            code_sems,
            code_sems,
        ],
        specs=[vmem, vmem, hbm],
        out_specs=hbm,
        elements=elements,
    )(copies, code_potential, in_hbm(scores))
    updated_codebook = call(
        functools.partial(refresh_kernel, math.log2(total_tokens)),
        jax.ShapeDtypeStruct((share, depth), f32),
        [
            pltpu.VMEM((total_tokens, depth), tokens.dtype),
            pltpu.VMEM((share, depth), codebook.dtype),
            pltpu.VMEM((share, LANES), f32),
            pltpu.SemaphoreType.DMA((total_tokens // CHUNK,)),
            pltpu.SemaphoreType.DMA,
        ],
        specs=[vmem, vmem, hbm, hbm],
        elements=elements,
        flops=4 * elements * depth,
    )(code_potential, all_potential, in_hbm(codebook), in_hbm(all_tokens))
    return (targets, updated_codebook)


def solution(mesh):
    return jax.shard_map(
        per_device,
        mesh=mesh,
        in_specs=(P("tok", None), P("code", None)),
        out_specs=(P("tok", "code"), P(("code", "tok"), None)),
        check_vma=False,
    )
```

```python
import functools
import math

import jax
import jax.numpy as jnp
from jax import lax
from jax.experimental import pallas as pl
from jax.experimental.pallas import tpu as pltpu
from jax.sharding import PartitionSpec as P

ITERS = 3


sharpness_factor = 2.5
rms_epsilon = 1e-06

LANES = 128
CHUNK = 512
AHEAD = 3
MIB = 1 << 20

score_scale = sharpness_factor * math.log2(math.e)


def lse2(values, axis):
    top = jnp.max(values, axis=axis, keepdims=True)
    total = jnp.sum(jnp.exp2(values - top), axis=axis)
    return jnp.squeeze(top, axis) + jnp.log2(total)


def as_column(row):
    return jnp.broadcast_to(row, (LANES, LANES)).T


def tile(k):
    return pl.ds(pl.multiple_of(k * LANES, LANES), LANES)


def column_lse(scores, potential, k):
    values = scores[:, tile(k)]
    if potential is not None:
        values = values + potential[...]
    values = values.reshape(values.shape[0] // 8, 8, LANES)
    top = jnp.max(values, axis=0)
    total = jnp.sum(jnp.exp2(values - top[None]), axis=0)
    most = jnp.max(top, axis=0, keepdims=True)
    total = jnp.sum(total * jnp.exp2(top - most), axis=0, keepdims=True)
    return most + jnp.log2(total)


def send_copies(local, out):
    for d in range(out.shape[0]):
        out[d] = local[...]


def send_copies(local, out):
    for d in range(out.shape[0]):
        out[d] = local[...]


def chunk_copies(source, held, sems, axis=0):
    copies = []
    for k in range(source.shape[axis] // CHUNK):
        part = (slice(None),) * axis + (pl.ds(k * CHUNK, CHUNK),)
        copies.append(pltpu.make_async_copy(source.at[part], held.at[part], sems.at[k]))
    return copies


def scores_kernel(tokens, codebook, scores, out, held, rows, local, sems, rows_sem):
    copies = chunk_copies(codebook, held, sems)
    rows_copy = pltpu.make_async_copy(tokens, rows, rows_sem)
    rows_copy.start()
    for copy in copies[:AHEAD]:
        copy.start()
    rows_copy.wait()
    for k in range(len(copies) + 1):
        if k < len(copies):
            copies[k].wait()
            if k + AHEAD < len(copies):
                copies[k + AHEAD].start()
            scores[:, pl.ds(k * CHUNK, CHUNK)] = (
                lax.dot_general(
                    rows[...],
                    held[pl.ds(k * CHUNK, CHUNK), :],
                    (((1,), (1,)), ((), ())),
                    preferred_element_type=jnp.float32,
                )
                * score_scale
            )
        if k > 0:
            for j in range((k - 1) * CHUNK // LANES, k * CHUNK // LANES):
                local[pl.ds(j, 1), :] = column_lse(scores, None, j)
    send_copies(local, out)


def columns_kernel(shift, received, scores, out, column, local):
    potential = -shift - lse2(received[...], 0)
    for h in range(potential.shape[0]):
        column[pl.ds(h * LANES, LANES), :] = as_column(potential[h : h + 1, :])

    def step(k, carry):
        local[pl.ds(k, 1), :] = column_lse(scores, column, k)
        return carry

    lax.fori_loop(0, local.shape[0], step, 0, unroll=8)
    send_copies(local, out)


def rows_kernel(shift, received, scores, out, potential):
    potential[...] = -shift - lse2(received[...], 0)
    tiles = potential.shape[0]
    partials = []
    for h in range(out.shape[1]):
        rows = pl.ds(h * LANES, LANES)

        def values(k):
            return scores[rows, tile(k)] + potential[pl.ds(k, 1), :]

        top = lax.fori_loop(
            0, tiles, lambda k, top: jnp.maximum(top, values(k)), values(0), unroll=8
        )
        total = lax.fori_loop(
            0,
            tiles,
            lambda k, total: total + jnp.exp2(values(k) - top),
            jnp.zeros((LANES, LANES), jnp.float32),
            unroll=8,
        )
        partials.append((top, total))
    for h, (top, total) in enumerate(partials):
        top = top.T
        most = jnp.max(top, axis=0, keepdims=True)
        total = jnp.sum(total.T * jnp.exp2(top - most), axis=0, keepdims=True)
        local = most + jnp.log2(total)
        for d in range(out.shape[0]):
            out[d, pl.ds(h, 1), :] = local


def token_potential_kernel(shift, received, out):
    potential = -shift - lse2(received[...], 0)
    for d in range(out.shape[0]):
        out[d] = potential


def targets_kernel(
    scale, token_potential, code_potential, scores, out, column, panel, held, sems, out_sems
):
    copies = chunk_copies(scores, panel, sems, 1)
    for copy in copies:
        copy.start()
    for h in range(token_potential.shape[1]):
        column[pl.ds(h * LANES, LANES), :] = as_column(token_potential[0, pl.ds(h, 1), :]) + scale
    out_copies = chunk_copies(held, out, out_sems, 1)
    for k in range(len(copies)):
        copies[k].wait()
        for j in range(k * CHUNK // LANES, (k + 1) * CHUNK // LANES):
            held[:, tile(j)] = jnp.exp2(
                panel[:, tile(j)] + column[...] + code_potential[pl.ds(j, 1), :]
            ).astype(held.dtype)
        out_copies[k].start()
    for copy in out_copies:
        copy.wait()


def own_code_copy(codebook, codes, sem):
    share = codes.shape[0]
    start = pl.multiple_of(lax.axis_index("tok") * share, share)
    return pltpu.make_async_copy(codebook.at[pl.ds(start, share)], codes, sem)


def refresh_kernel(
    scale, code_potential, potential, codebook, tokens, out, held, codes, column, sems, own_sem
):
    own = own_code_copy(codebook, codes, own_sem)
    copies = chunk_copies(tokens, held, sems)
    own.start()
    for copy in copies[:AHEAD]:
        copy.start()
    halves, tiles = potential.shape[1], codes.shape[0] // LANES
    for h in range(tiles):
        row = code_potential[pl.ds(lax.axis_index("tok") * tiles + h, 1), :]
        column[pl.ds(h * LANES, LANES), :] = as_column(row) + scale
    own.wait()

    def part(k):
        return held[pl.ds(k * CHUNK, CHUNK), :]

    def chunk_scores(k):
        copies[k].wait()
        if k + AHEAD < len(copies):
            copies[k + AHEAD].start()
        return lax.dot_general(
            codes[...], part(k), (((1,), (1,)), ((), ())), preferred_element_type=jnp.float32
        )

    assigned = jnp.zeros(out.shape, jnp.float32)
    scores = chunk_scores(0)
    for k in range(len(copies)):
        ahead = chunk_scores(k + 1) if k + 1 < len(copies) else None
        weights = []
        for j in range(CHUNK // LANES):
            at = k * CHUNK // LANES + j
            row = potential[at // halves, pl.ds(at % halves, 1), :]
            values = scores[:, j * LANES : (j + 1) * LANES] * score_scale + column[...] + row
            weights.append(jnp.exp2(values).astype(held.dtype))
        assigned += jnp.dot(
            jnp.concatenate(weights, axis=1), part(k), preferred_element_type=jnp.float32
        )
        scores = ahead
    mixed = codes[...].astype(jnp.float32) + assigned
    out[...] = mixed * lax.rsqrt(
        jnp.mean(mixed * mixed, axis=1, keepdims=True) + rms_epsilon
    )


def in_vmem(array):
    return pltpu.with_memory_space_constraint(array, pltpu.VMEM)


def in_hbm(array):
    return pltpu.with_memory_space_constraint(array, pltpu.HBM)


def call(kernel, out_shape, scratch=(), specs=None, out_specs=None, limit=24, elements=0, flops=0):
    vmem = pl.BlockSpec(memory_space=pltpu.VMEM)
    return pl.pallas_call(
        kernel,
        out_shape=out_shape,
        in_specs=specs,
        out_specs=out_specs if out_specs is not None else jax.tree.map(lambda _: vmem, out_shape),
        scratch_shapes=list(scratch),
        compiler_params=pltpu.CompilerParams(vmem_limit_bytes=limit * MIB),
        cost_estimate=pl.CostEstimate(
            flops=flops + 4 * elements, transcendentals=elements, bytes_accessed=4 * elements
        ),
    )


def per_device(tokens, codebook):
    tok_size, code_size = lax.axis_size("tok"), lax.axis_size("code")
    tok_rows, depth = tokens.shape
    code_rows = codebook.shape[0]
    total_tokens = tok_rows * tok_size
    total_codes = code_rows * code_size
    share = code_rows // tok_size
    row_tiles, code_tiles = tok_rows // LANES, code_rows // LANES
    elements = tok_rows * code_rows
    f32 = jnp.float32
    vmem = pl.BlockSpec(memory_space=pltpu.VMEM)
    hbm = pl.BlockSpec(memory_space=pltpu.HBM)
    to_tok = jax.ShapeDtypeStruct((tok_size, code_tiles, LANES), f32)
    to_code = jax.ShapeDtypeStruct((code_size, row_tiles, LANES), f32)
    column = pltpu.VMEM((tok_rows, LANES), f32)

    def exchange(copies, axis):
        return lax.all_to_all(copies, axis, 0, 0)

    all_tokens = lax.all_gather(tokens, "tok", axis=0, tiled=True)

    scores, copies = call(
        scores_kernel,
        (pltpu.VMEM((tok_rows, code_rows), f32), to_tok),
        [
            pltpu.VMEM((code_rows, depth), codebook.dtype),
            pltpu.VMEM((tok_rows, depth), tokens.dtype),
            pltpu.VMEM((code_tiles, LANES), f32),
            pltpu.SemaphoreType.DMA((code_rows // CHUNK,)),
            pltpu.SemaphoreType.DMA,
        ],
        specs=[hbm, hbm],
        elements=elements,
        flops=2 * elements * depth,
    )(in_hbm(tokens), in_hbm(codebook))
    for step in range(ITERS):
        last = step == ITERS - 1
        potential = pltpu.VMEM((code_tiles, LANES), f32)
        copies, *code_potential = call(
            functools.partial(rows_kernel, math.log2(total_codes)),
            (to_code, potential) if last else (to_code,),
            [] if last else [potential],
            specs=[vmem, vmem],
            elements=elements,
        )(exchange(copies, "tok"), in_vmem(scores))
        received = exchange(copies, "code")
        if not last:
            copies = call(
                functools.partial(columns_kernel, math.log2(total_tokens)),
                to_tok,
                [column, potential],
                specs=[vmem, vmem],
                elements=elements,
            )(received, in_vmem(scores))
    (code_potential,) = code_potential

    copies = call(
        functools.partial(token_potential_kernel, math.log2(total_tokens)),
        jax.ShapeDtypeStruct((tok_size, row_tiles, LANES), f32),
        specs=[vmem],
    )(received)
    all_potential = exchange(copies, "tok")
    code_sems = pltpu.SemaphoreType.DMA((code_rows // CHUNK,))
    targets = call(
        functools.partial(targets_kernel, math.log2(total_tokens)),
        jax.ShapeDtypeStruct((tok_rows, code_rows), jnp.bfloat16),
        [
            column,
            pltpu.VMEM((tok_rows, code_rows), f32),
            pltpu.VMEM((tok_rows, code_rows), jnp.bfloat16),
            code_sems,
            code_sems,
        ],
        specs=[vmem, vmem, hbm],
        out_specs=hbm,
        elements=elements,
    )(copies, code_potential, in_hbm(scores))
    updated_codebook = call(
        functools.partial(refresh_kernel, math.log2(total_tokens)),
        jax.ShapeDtypeStruct((share, depth), f32),
        [
            pltpu.VMEM((total_tokens, depth), tokens.dtype),
            pltpu.VMEM((share, depth), codebook.dtype),
            pltpu.VMEM((share, LANES), f32),
            pltpu.SemaphoreType.DMA((total_tokens // CHUNK,)),
            pltpu.SemaphoreType.DMA,
        ],
        specs=[vmem, vmem, hbm, hbm],
        elements=elements,
        flops=4 * elements * depth,
    )(code_potential, all_potential, in_hbm(codebook), in_hbm(all_tokens))
    return (targets, updated_codebook)


def solution(mesh):
    return jax.shard_map(
        per_device,
        mesh=mesh,
        in_specs=(P("tok", None), P("code", None)),
        out_specs=(P("tok", "code"), P(("code", "tok"), None)),
        check_vma=False,
    )
```

```python
import functools
import math

import jax
import jax.numpy as jnp
from jax import lax
from jax.experimental import pallas as pl
from jax.experimental.pallas import tpu as pltpu
from jax.sharding import PartitionSpec as P

ITERS = 3


sharpness_factor = 2.5
rms_epsilon = 1e-06

LANES = 128
CHUNK = 1024
AHEAD = 2
MIB = 1 << 20

score_scale = sharpness_factor * math.log2(math.e)


def lse2(values, axis):
    top = jnp.max(values, axis=axis, keepdims=True)
    total = jnp.sum(jnp.exp2(values - top), axis=axis)
    return jnp.squeeze(top, axis) + jnp.log2(total)


def as_column(row):
    return jnp.broadcast_to(row, (LANES, LANES)).T


def tile(k):
    return pl.ds(pl.multiple_of(k * LANES, LANES), LANES)


def column_lse(scores, potential, k):
    values = scores[:, tile(k)]
    if potential is not None:
        values = values + potential[...]
    values = values.reshape(values.shape[0] // 8, 8, LANES)
    top = jnp.max(values, axis=0)
    total = jnp.sum(jnp.exp2(values - top[None]), axis=0)
    most = jnp.max(top, axis=0, keepdims=True)
    total = jnp.sum(total * jnp.exp2(top - most), axis=0, keepdims=True)
    return most + jnp.log2(total)


def send_copies(local, out):
    for d in range(out.shape[0]):
        out[d] = local[...]


def send_copies(local, out):
    for d in range(out.shape[0]):
        out[d] = local[...]


def chunk_copies(source, held, sems, axis=0):
    copies = []
    for k in range(source.shape[axis] // CHUNK):
        part = (slice(None),) * axis + (pl.ds(k * CHUNK, CHUNK),)
        copies.append(pltpu.make_async_copy(source.at[part], held.at[part], sems.at[k]))
    return copies


def scores_kernel(tokens, codebook, scores, out, held, rows, local, sems, rows_sem):
    copies = chunk_copies(codebook, held, sems)
    rows_copy = pltpu.make_async_copy(tokens, rows, rows_sem)
    rows_copy.start()
    for copy in copies[:AHEAD]:
        copy.start()
    rows_copy.wait()
    for k in range(len(copies) + 1):
        if k < len(copies):
            copies[k].wait()
            if k + AHEAD < len(copies):
                copies[k + AHEAD].start()
            scores[:, pl.ds(k * CHUNK, CHUNK)] = (
                lax.dot_general(
                    rows[...],
                    held[pl.ds(k * CHUNK, CHUNK), :],
                    (((1,), (1,)), ((), ())),
                    preferred_element_type=jnp.float32,
                )
                * score_scale
            )
        if k > 0:
            for j in range((k - 1) * CHUNK // LANES, k * CHUNK // LANES):
                local[pl.ds(j, 1), :] = column_lse(scores, None, j)
    send_copies(local, out)


def columns_kernel(shift, received, scores, out, column, local):
    potential = -shift - lse2(received[...], 0)
    for h in range(potential.shape[0]):
        column[pl.ds(h * LANES, LANES), :] = as_column(potential[h : h + 1, :])

    def step(k, carry):
        local[pl.ds(k, 1), :] = column_lse(scores, column, k)
        return carry

    lax.fori_loop(0, local.shape[0], step, 0, unroll=8)
    send_copies(local, out)


def rows_kernel(shift, received, scores, out, potential):
    potential[...] = -shift - lse2(received[...], 0)
    tiles = potential.shape[0]
    partials = []
    for h in range(out.shape[1]):
        rows = pl.ds(h * LANES, LANES)

        def values(k):
            return scores[rows, tile(k)] + potential[pl.ds(k, 1), :]

        top = lax.fori_loop(
            0, tiles, lambda k, top: jnp.maximum(top, values(k)), values(0), unroll=8
        )
        total = lax.fori_loop(
            0,
            tiles,
            lambda k, total: total + jnp.exp2(values(k) - top),
            jnp.zeros((LANES, LANES), jnp.float32),
            unroll=8,
        )
        partials.append((top, total))
    for h, (top, total) in enumerate(partials):
        top = top.T
        most = jnp.max(top, axis=0, keepdims=True)
        total = jnp.sum(total.T * jnp.exp2(top - most), axis=0, keepdims=True)
        local = most + jnp.log2(total)
        for d in range(out.shape[0]):
            out[d, pl.ds(h, 1), :] = local


def last_rows_kernel(shift, received, scores, tokens, out, potential, first_tokens, sem):
    copy = pltpu.make_async_copy(
        tokens.at[pl.ds(0, first_tokens.shape[0])], first_tokens, sem
    )
    copy.start()
    rows_kernel(shift, received, scores, out, potential)
    copy.wait()


def own_code_copy(codebook, codes, sem):
    share = codes.shape[0]
    start = pl.multiple_of(lax.axis_index("tok") * share, share)
    return pltpu.make_async_copy(codebook.at[pl.ds(start, share)], codes, sem)


def targets_kernel(
    scale, received, code_potential, scores, codebook, tokens, first_tokens,
    out, targets, own_scores, last_tokens,
    panel, column, own_column, codes, own_sem, sems, out_sems,
):
    own = own_code_copy(codebook, codes, own_sem)
    own.start()
    first = first_tokens.shape[0]
    copies = chunk_copies(tokens.at[pl.ds(first, last_tokens.shape[0])], last_tokens, sems)
    for copy in copies:
        copy.start()
    potential = -scale - lse2(received[...], 0)
    for d in range(out.shape[0]):
        out[d] = potential
    tiles = codes.shape[0] // LANES
    for h in range(tiles):
        row = code_potential[pl.ds(lax.axis_index("tok") * tiles + h, 1), :]
        own_column[pl.ds(h * LANES, LANES), :] = as_column(row) + scale
    for h in range(potential.shape[0]):
        column[pl.ds(h * LANES, LANES), :] = as_column(potential[h : h + 1, :]) + scale
    own.wait()
    out_copies = chunk_copies(panel, targets, out_sems, 1)
    for k in range(len(out_copies)):
        if k * CHUNK < first:
            part = first_tokens[pl.ds(k * CHUNK, CHUNK), :]
        else:
            copies[k - first // CHUNK].wait()
            part = last_tokens[pl.ds(k * CHUNK - first, CHUNK), :]
        values = lax.dot_general(
            codes[...], part, (((1,), (1,)), ((), ())), preferred_element_type=jnp.float32
        )
        for j in range(CHUNK // LANES):
            at = k * CHUNK // LANES + j
            panel[:, tile(at)] = jnp.exp2(
                scores[:, tile(at)] + column[...] + code_potential[pl.ds(at, 1), :]
            ).astype(panel.dtype)
            own_scores[:, tile(at)] = (
                values[:, j * LANES : (j + 1) * LANES] * score_scale + own_column[...]
            )
        out_copies[k].start()
    for copy in out_copies:
        copy.wait()


def refresh_kernel(potential, codebook, scores, first_tokens, last_tokens, out, codes, own_sem):
    own = own_code_copy(codebook, codes, own_sem)
    own.start()
    halves = potential.shape[1]
    assigned = jnp.zeros(out.shape, jnp.float32)
    at = 0
    for tokens in (first_tokens, last_tokens):
        for k in range(tokens.shape[0] // CHUNK):
            weights = []
            for j in range(CHUNK // LANES):
                row = potential[at // halves, pl.ds(at % halves, 1), :]
                weights.append(jnp.exp2(scores[:, tile(at)] + row).astype(tokens.dtype))
                at += 1
            assigned += jnp.dot(
                jnp.concatenate(weights, axis=1),
                tokens[pl.ds(k * CHUNK, CHUNK), :],
                preferred_element_type=jnp.float32,
            )
    own.wait()
    mixed = codes[...].astype(jnp.float32) + assigned
    out[...] = mixed * lax.rsqrt(
        jnp.mean(mixed * mixed, axis=1, keepdims=True) + rms_epsilon
    )


def in_vmem(array):
    return pltpu.with_memory_space_constraint(array, pltpu.VMEM)


def in_hbm(array):
    return pltpu.with_memory_space_constraint(array, pltpu.HBM)


def call(kernel, out_shape, scratch=(), specs=None, out_specs=None, limit=24, elements=0, flops=0):
    vmem = pl.BlockSpec(memory_space=pltpu.VMEM)
    return pl.pallas_call(
        kernel,
        out_shape=out_shape,
        in_specs=specs,
        out_specs=out_specs if out_specs is not None else jax.tree.map(lambda _: vmem, out_shape),
        scratch_shapes=list(scratch),
        compiler_params=pltpu.CompilerParams(vmem_limit_bytes=limit * MIB),
        cost_estimate=pl.CostEstimate(
            flops=flops + 4 * elements, transcendentals=elements, bytes_accessed=4 * elements
        ),
    )


def per_device(tokens, codebook):
    tok_size, code_size = lax.axis_size("tok"), lax.axis_size("code")
    tok_rows, depth = tokens.shape
    code_rows = codebook.shape[0]
    total_tokens = tok_rows * tok_size
    total_codes = code_rows * code_size
    share = code_rows // tok_size
    row_tiles, code_tiles = tok_rows // LANES, code_rows // LANES
    elements = tok_rows * code_rows
    f32 = jnp.float32
    vmem = pl.BlockSpec(memory_space=pltpu.VMEM)
    hbm = pl.BlockSpec(memory_space=pltpu.HBM)
    to_tok = jax.ShapeDtypeStruct((tok_size, code_tiles, LANES), f32)
    to_code = jax.ShapeDtypeStruct((code_size, row_tiles, LANES), f32)
    column = pltpu.VMEM((tok_rows, LANES), f32)

    def exchange(copies, axis):
        return lax.all_to_all(copies, axis, 0, 0)

    all_tokens = lax.all_gather(tokens, "tok", axis=0, tiled=True)

    scores, copies = call(
        scores_kernel,
        (pltpu.VMEM((tok_rows, code_rows), f32), to_tok),
        [
            pltpu.VMEM((code_rows, depth), codebook.dtype),
            pltpu.VMEM((tok_rows, depth), tokens.dtype),
            pltpu.VMEM((code_tiles, LANES), f32),
            pltpu.SemaphoreType.DMA((code_rows // CHUNK,)),
            pltpu.SemaphoreType.DMA,
        ],
        specs=[hbm, hbm],
        elements=elements,
        flops=2 * elements * depth,
    )(in_hbm(tokens), in_hbm(codebook))
    potential = pltpu.VMEM((code_tiles, LANES), f32)
    half_tokens = pltpu.VMEM((total_tokens // 2, depth), tokens.dtype)
    for step in range(ITERS):
        received = exchange(copies, "tok")
        if step < ITERS - 1:
            copies = call(
                functools.partial(rows_kernel, math.log2(total_codes)),
                to_code,
                [potential],
                specs=[vmem, vmem],
                elements=elements,
            )(received, in_vmem(scores))
            received = exchange(copies, "code")
            copies = call(
                functools.partial(columns_kernel, math.log2(total_tokens)),
                to_tok,
                [column, potential],
                specs=[vmem, vmem],
                elements=elements,
            )(received, in_vmem(scores))
        else:
            copies, code_potential, first_tokens = call(
                functools.partial(last_rows_kernel, math.log2(total_codes)),
                (to_code, potential, half_tokens),
                [pltpu.SemaphoreType.DMA],
                specs=[vmem, vmem, hbm],
                elements=elements,
            )(received, in_vmem(scores), in_hbm(all_tokens))
            received = exchange(copies, "code")

    held_codes = pltpu.VMEM((share, depth), codebook.dtype)
    copies, targets, own_scores, last_tokens = call(
        functools.partial(targets_kernel, math.log2(total_tokens)),
        (
            jax.ShapeDtypeStruct((tok_size, row_tiles, LANES), f32),
            jax.ShapeDtypeStruct((tok_rows, code_rows), jnp.bfloat16),
            pltpu.VMEM((share, total_tokens), f32),
            half_tokens,
        ),
        [
            pltpu.VMEM((tok_rows, code_rows), jnp.bfloat16),
            column,
            pltpu.VMEM((share, LANES), f32),
            held_codes,
            pltpu.SemaphoreType.DMA,
            pltpu.SemaphoreType.DMA((total_tokens // 2 // CHUNK,)),
            pltpu.SemaphoreType.DMA((code_rows // CHUNK,)),
        ],
        specs=[vmem, vmem, vmem, hbm, hbm, vmem],
        out_specs=(vmem, hbm, vmem, vmem),
        elements=2 * elements,
        flops=2 * elements * depth,
    )(
        received,
        in_vmem(code_potential),
        in_vmem(scores),
        in_hbm(codebook),
        in_hbm(all_tokens),
        in_vmem(first_tokens),
    )
    all_potential = exchange(copies, "tok")
    updated_codebook = call(
        refresh_kernel,
        jax.ShapeDtypeStruct((share, depth), f32),
        [held_codes, pltpu.SemaphoreType.DMA],
        specs=[vmem, hbm, vmem, vmem, vmem],
        elements=elements,
        flops=2 * elements * depth,
    )(
        all_potential,
        in_hbm(codebook),
        in_vmem(own_scores),
        in_vmem(first_tokens),
        in_vmem(last_tokens),
    )
    return (targets, updated_codebook)


def solution(mesh):
    return jax.shard_map(
        per_device,
        mesh=mesh,
        in_specs=(P("tok", None), P("code", None)),
        out_specs=(P("tok", "code"), P(("code", "tok"), None)),
        check_vma=False,
    )
```

```python
import functools
import math

import jax
import jax.numpy as jnp
from jax import lax
from jax.experimental import pallas as pl
from jax.experimental.pallas import tpu as pltpu
from jax.sharding import PartitionSpec as P

ITERS = 3


sharpness_factor = 2.5
rms_epsilon = 1e-06

LANES = 128
CHUNK = 512
AHEAD = 3
CODE_CHUNK = 1024
CODE_AHEAD = 2
MIB = 1 << 20

score_scale = sharpness_factor * math.log2(math.e)


def lse2(values, axis):
    top = jnp.max(values, axis=axis, keepdims=True)
    total = jnp.sum(jnp.exp2(values - top), axis=axis)
    return jnp.squeeze(top, axis) + jnp.log2(total)


def as_column(row):
    return jnp.broadcast_to(row, (LANES, LANES)).T


def tile(k):
    return pl.ds(pl.multiple_of(k * LANES, LANES), LANES)


def column_lse(scores, potential, k):
    values = scores[:, tile(k)]
    if potential is not None:
        values = values + potential[...]
    values = values.reshape(values.shape[0] // 8, 8, LANES)
    top = jnp.max(values, axis=0)
    total = jnp.sum(jnp.exp2(values - top[None]), axis=0)
    most = jnp.max(top, axis=0, keepdims=True)
    total = jnp.sum(total * jnp.exp2(top - most), axis=0, keepdims=True)
    return most + jnp.log2(total)


def send_copies(local, out):
    for d in range(out.shape[0]):
        out[d] = local[...]


def send_copies(local, out):
    for d in range(out.shape[0]):
        out[d] = local[...]


def chunk_copies(source, held, sems, axis=0, size=CHUNK):
    copies = []
    for k in range(source.shape[axis] // size):
        part = (slice(None),) * axis + (pl.ds(k * size, size),)
        copies.append(pltpu.make_async_copy(source.at[part], held.at[part], sems.at[k]))
    return copies


def scores_of(left, right):
    return lax.dot_general(
        left, right, (((1,), (1,)), ((), ())), preferred_element_type=jnp.float32
    ).T


def scores_kernel(tokens, codebook, scores, out, held, rows, local, sems, rows_sem):
    size = CODE_CHUNK
    copies = chunk_copies(codebook, held, sems, 0, size)
    rows_copy = pltpu.make_async_copy(tokens, rows, rows_sem)
    rows_copy.start()
    for copy in copies[:CODE_AHEAD]:
        copy.start()
    rows_copy.wait()
    for k in range(len(copies) + 1):
        if k < len(copies):
            copies[k].wait()
            if k + CODE_AHEAD < len(copies):
                copies[k + CODE_AHEAD].start()
            part = pl.ds(k * size, size)
            scores[:, part] = scores_of(held[part, :], rows[...]) * score_scale
        if k > 0:
            for j in range((k - 1) * size // LANES, k * size // LANES):
                local[pl.ds(j, 1), :] = column_lse(scores, None, j)
    send_copies(local, out)


def columns_kernel(shift, received, scores, out, column, local):
    potential = -shift - lse2(received[...], 0)
    for h in range(potential.shape[0]):
        column[pl.ds(h * LANES, LANES), :] = as_column(potential[h : h + 1, :])

    def step(k, carry):
        local[pl.ds(k, 1), :] = column_lse(scores, column, k)
        return carry

    lax.fori_loop(0, local.shape[0], step, 0, unroll=8)
    send_copies(local, out)


def rows_kernel(shift, received, scores, out, potential):
    potential[...] = -shift - lse2(received[...], 0)
    tiles = potential.shape[0]
    partials = []
    for h in range(out.shape[1]):
        rows = pl.ds(h * LANES, LANES)

        def values(k):
            return scores[rows, tile(k)] + potential[pl.ds(k, 1), :]

        top = lax.fori_loop(
            0, tiles, lambda k, top: jnp.maximum(top, values(k)), values(0), unroll=8
        )
        total = lax.fori_loop(
            0,
            tiles,
            lambda k, total: total + jnp.exp2(values(k) - top),
            jnp.zeros((LANES, LANES), jnp.float32),
            unroll=8,
        )
        partials.append((top, total))
    for h, (top, total) in enumerate(partials):
        top = top.T
        most = jnp.max(top, axis=0, keepdims=True)
        total = jnp.sum(total.T * jnp.exp2(top - most), axis=0, keepdims=True)
        local = most + jnp.log2(total)
        for d in range(out.shape[0]):
            out[d, pl.ds(h, 1), :] = local


def token_potential_kernel(shift, received, out):
    potential = -shift - lse2(received[...], 0)
    for d in range(out.shape[0]):
        out[d] = potential


def targets_kernel(
    scale, token_potential, code_potential, scores, out, column, panel, held, sems, out_sems
):
    copies = chunk_copies(scores, panel, sems, 1)
    for copy in copies:
        copy.start()
    for h in range(token_potential.shape[1]):
        column[pl.ds(h * LANES, LANES), :] = as_column(token_potential[0, pl.ds(h, 1), :]) + scale
    out_copies = chunk_copies(held, out, out_sems, 1)
    for k in range(len(copies)):
        copies[k].wait()
        for j in range(k * CHUNK // LANES, (k + 1) * CHUNK // LANES):
            held[:, tile(j)] = jnp.exp2(
                panel[:, tile(j)] + column[...] + code_potential[pl.ds(j, 1), :]
            ).astype(held.dtype)
        out_copies[k].start()
    for copy in out_copies:
        copy.wait()


def own_code_copy(codebook, codes, sem):
    share = codes.shape[0]
    start = pl.multiple_of(lax.axis_index("tok") * share, share)
    return pltpu.make_async_copy(codebook.at[pl.ds(start, share)], codes, sem)


def refresh_kernel(
    scale, code_potential, potential, codebook, tokens, out, held, codes, column, sems, own_sem
):
    own = own_code_copy(codebook, codes, own_sem)
    copies = chunk_copies(tokens, held, sems)
    own.start()
    for copy in copies[:AHEAD]:
        copy.start()
    halves, tiles = potential.shape[1], codes.shape[0] // LANES
    for h in range(tiles):
        row = code_potential[pl.ds(lax.axis_index("tok") * tiles + h, 1), :]
        column[pl.ds(h * LANES, LANES), :] = as_column(row) + scale
    own.wait()

    def part(k):
        return held[pl.ds(k * CHUNK, CHUNK), :]

    def chunk_scores(k):
        copies[k].wait()
        if k + AHEAD < len(copies):
            copies[k + AHEAD].start()
        return scores_of(part(k), codes[...])

    assigned = jnp.zeros(out.shape, jnp.float32)
    scores = chunk_scores(0)
    for k in range(len(copies)):
        ahead = chunk_scores(k + 1) if k + 1 < len(copies) else None
        weights = []
        for j in range(CHUNK // LANES):
            at = k * CHUNK // LANES + j
            row = potential[at // halves, pl.ds(at % halves, 1), :]
            values = scores[:, j * LANES : (j + 1) * LANES] * score_scale + column[...] + row
            weights.append(jnp.exp2(values).astype(held.dtype))
        assigned += jnp.dot(
            jnp.concatenate(weights, axis=1), part(k), preferred_element_type=jnp.float32
        )
        scores = ahead
    mixed = codes[...].astype(jnp.float32) + assigned
    out[...] = mixed * lax.rsqrt(
        jnp.mean(mixed * mixed, axis=1, keepdims=True) + rms_epsilon
    )


def in_vmem(array):
    return pltpu.with_memory_space_constraint(array, pltpu.VMEM)


def in_hbm(array):
    return pltpu.with_memory_space_constraint(array, pltpu.HBM)


def call(kernel, out_shape, scratch=(), specs=None, out_specs=None, limit=24, elements=0, flops=0):
    vmem = pl.BlockSpec(memory_space=pltpu.VMEM)
    return pl.pallas_call(
        kernel,
        out_shape=out_shape,
        in_specs=specs,
        out_specs=out_specs if out_specs is not None else jax.tree.map(lambda _: vmem, out_shape),
        scratch_shapes=list(scratch),
        compiler_params=pltpu.CompilerParams(vmem_limit_bytes=limit * MIB),
        cost_estimate=pl.CostEstimate(
            flops=flops + 4 * elements, transcendentals=elements, bytes_accessed=4 * elements
        ),
    )


def per_device(tokens, codebook):
    tok_size, code_size = lax.axis_size("tok"), lax.axis_size("code")
    tok_rows, depth = tokens.shape
    code_rows = codebook.shape[0]
    total_tokens = tok_rows * tok_size
    total_codes = code_rows * code_size
    share = code_rows // tok_size
    row_tiles, code_tiles = tok_rows // LANES, code_rows // LANES
    elements = tok_rows * code_rows
    f32 = jnp.float32
    vmem = pl.BlockSpec(memory_space=pltpu.VMEM)
    hbm = pl.BlockSpec(memory_space=pltpu.HBM)
    to_tok = jax.ShapeDtypeStruct((tok_size, code_tiles, LANES), f32)
    to_code = jax.ShapeDtypeStruct((code_size, row_tiles, LANES), f32)
    column = pltpu.VMEM((tok_rows, LANES), f32)

    def exchange(copies, axis):
        return lax.all_to_all(copies, axis, 0, 0)

    all_tokens = lax.all_gather(tokens, "tok", axis=0, tiled=True)

    scores, copies = call(
        scores_kernel,
        (pltpu.VMEM((tok_rows, code_rows), f32), to_tok),
        [
            pltpu.VMEM((code_rows, depth), codebook.dtype),
            pltpu.VMEM((tok_rows, depth), tokens.dtype),
            pltpu.VMEM((code_tiles, LANES), f32),
            pltpu.SemaphoreType.DMA((code_rows // CODE_CHUNK,)),
            pltpu.SemaphoreType.DMA,
        ],
        specs=[hbm, hbm],
        elements=elements,
        flops=2 * elements * depth,
    )(in_hbm(tokens), in_hbm(codebook))
    for step in range(ITERS):
        last = step == ITERS - 1
        potential = pltpu.VMEM((code_tiles, LANES), f32)
        copies, *code_potential = call(
            functools.partial(rows_kernel, math.log2(total_codes)),
            (to_code, potential) if last else (to_code,),
            [] if last else [potential],
            specs=[vmem, vmem],
            elements=elements,
        )(exchange(copies, "tok"), in_vmem(scores))
        received = exchange(copies, "code")
        if not last:
            copies = call(
                functools.partial(columns_kernel, math.log2(total_tokens)),
                to_tok,
                [column, potential],
                specs=[vmem, vmem],
                elements=elements,
            )(received, in_vmem(scores))
    (code_potential,) = code_potential

    copies = call(
        functools.partial(token_potential_kernel, math.log2(total_tokens)),
        jax.ShapeDtypeStruct((tok_size, row_tiles, LANES), f32),
        specs=[vmem],
    )(received)
    all_potential = exchange(copies, "tok")
    code_sems = pltpu.SemaphoreType.DMA((code_rows // CHUNK,))
    targets = call(
        functools.partial(targets_kernel, math.log2(total_tokens)),
        jax.ShapeDtypeStruct((tok_rows, code_rows), jnp.bfloat16),
        [
            column,
            pltpu.VMEM((tok_rows, code_rows), f32),
            pltpu.VMEM((tok_rows, code_rows), jnp.bfloat16),
            code_sems,
            code_sems,
        ],
        specs=[vmem, vmem, hbm],
        out_specs=hbm,
        elements=elements,
    )(copies, code_potential, in_hbm(scores))
    updated_codebook = call(
        functools.partial(refresh_kernel, math.log2(total_tokens)),
        jax.ShapeDtypeStruct((share, depth), f32),
        [
            pltpu.VMEM((total_tokens, depth), tokens.dtype),
            pltpu.VMEM((share, depth), codebook.dtype),
            pltpu.VMEM((share, LANES), f32),
            pltpu.SemaphoreType.DMA((total_tokens // CHUNK,)),
            pltpu.SemaphoreType.DMA,
        ],
        specs=[vmem, vmem, hbm, hbm],
        elements=elements,
        flops=4 * elements * depth,
    )(code_potential, all_potential, in_hbm(codebook), in_hbm(all_tokens))
    return (targets, updated_codebook)


def solution(mesh):
    return jax.shard_map(
        per_device,
        mesh=mesh,
        in_specs=(P("tok", None), P("code", None)),
        out_specs=(P("tok", "code"), P(("code", "tok"), None)),
        check_vma=False,
    )
```

```python
import functools
import math

import jax
import jax.numpy as jnp
from jax import lax
from jax.experimental import pallas as pl
from jax.experimental.pallas import tpu as pltpu
from jax.sharding import PartitionSpec as P

ITERS = 3


sharpness_factor = 2.5
rms_epsilon = 1e-06

LANES = 128
CHUNK = 1024
DOT_CHUNK = 512
AHEAD = 2
MIB = 1 << 20

score_scale = sharpness_factor * math.log2(math.e)


def lse2(values, axis):
    top = jnp.max(values, axis=axis, keepdims=True)
    total = jnp.sum(jnp.exp2(values - top), axis=axis)
    return jnp.squeeze(top, axis) + jnp.log2(total)


def as_column(row):
    return jnp.broadcast_to(row, (LANES, LANES)).T


def tile(k):
    return pl.ds(pl.multiple_of(k * LANES, LANES), LANES)


def column_lse(scores, potential, k):
    values = scores[:, tile(k)]
    if potential is not None:
        values = values + potential[...]
    values = values.reshape(values.shape[0] // 8, 8, LANES)
    top = jnp.max(values, axis=0)
    total = jnp.sum(jnp.exp2(values - top[None]), axis=0)
    most = jnp.max(top, axis=0, keepdims=True)
    total = jnp.sum(total * jnp.exp2(top - most), axis=0, keepdims=True)
    return most + jnp.log2(total)


def send_copies(local, out):
    for d in range(out.shape[0]):
        out[d] = local[...]


def send_copies(local, out):
    for d in range(out.shape[0]):
        out[d] = local[...]


def chunk_copies(source, held, sems, axis=0):
    copies = []
    for k in range(source.shape[axis] // CHUNK):
        part = (slice(None),) * axis + (pl.ds(k * CHUNK, CHUNK),)
        copies.append(pltpu.make_async_copy(source.at[part], held.at[part], sems.at[k]))
    return copies


def scores_kernel(tokens, codebook, scores, out, held, rows, local, sems, rows_sem):
    copies = chunk_copies(codebook, held, sems)
    rows_copy = pltpu.make_async_copy(tokens, rows, rows_sem)
    rows_copy.start()
    for copy in copies[:AHEAD]:
        copy.start()
    rows_copy.wait()
    for k in range(len(copies) + 1):
        if k < len(copies):
            copies[k].wait()
            if k + AHEAD < len(copies):
                copies[k + AHEAD].start()
            scores[:, pl.ds(k * CHUNK, CHUNK)] = (
                lax.dot_general(
                    rows[...],
                    held[pl.ds(k * CHUNK, CHUNK), :],
                    (((1,), (1,)), ((), ())),
                    preferred_element_type=jnp.float32,
                )
                * score_scale
            )
        if k > 0:
            for j in range((k - 1) * CHUNK // LANES, k * CHUNK // LANES):
                local[pl.ds(j, 1), :] = column_lse(scores, None, j)
    send_copies(local, out)


def columns_kernel(shift, received, scores, out, column, local):
    potential = -shift - lse2(received[...], 0)
    for h in range(potential.shape[0]):
        column[pl.ds(h * LANES, LANES), :] = as_column(potential[h : h + 1, :])

    def step(k, carry):
        local[pl.ds(k, 1), :] = column_lse(scores, column, k)
        return carry

    lax.fori_loop(0, local.shape[0], step, 0, unroll=8)
    send_copies(local, out)


def rows_kernel(shift, received, scores, out, potential):
    potential[...] = -shift - lse2(received[...], 0)
    tiles = potential.shape[0]
    partials = []
    for h in range(out.shape[1]):
        rows = pl.ds(h * LANES, LANES)

        def values(k):
            return scores[rows, tile(k)] + potential[pl.ds(k, 1), :]

        top = lax.fori_loop(
            0, tiles, lambda k, top: jnp.maximum(top, values(k)), values(0), unroll=8
        )
        total = lax.fori_loop(
            0,
            tiles,
            lambda k, total: total + jnp.exp2(values(k) - top),
            jnp.zeros((LANES, LANES), jnp.float32),
            unroll=8,
        )
        partials.append((top, total))
    for h, (top, total) in enumerate(partials):
        top = top.T
        most = jnp.max(top, axis=0, keepdims=True)
        total = jnp.sum(total.T * jnp.exp2(top - most), axis=0, keepdims=True)
        local = most + jnp.log2(total)
        for d in range(out.shape[0]):
            out[d, pl.ds(h, 1), :] = local


def token_potential_kernel(shift, received, out):
    potential = -shift - lse2(received[...], 0)
    for d in range(out.shape[0]):
        out[d] = potential


def targets_kernel(
    scale, token_potential, code_potential, scores, out, column, panel, held, sems, out_sems
):
    copies = chunk_copies(scores, panel, sems, 1)
    for copy in copies:
        copy.start()
    for h in range(token_potential.shape[1]):
        column[pl.ds(h * LANES, LANES), :] = as_column(token_potential[0, pl.ds(h, 1), :]) + scale
    out_copies = chunk_copies(held, out, out_sems, 1)
    for k in range(len(copies)):
        copies[k].wait()
        for j in range(k * CHUNK // LANES, (k + 1) * CHUNK // LANES):
            held[:, tile(j)] = jnp.exp2(
                panel[:, tile(j)] + column[...] + code_potential[pl.ds(j, 1), :]
            ).astype(held.dtype)
        out_copies[k].start()
    for copy in out_copies:
        copy.wait()


def own_code_copy(codebook, codes, sem):
    share = codes.shape[0]
    start = pl.multiple_of(lax.axis_index("tok") * share, share)
    return pltpu.make_async_copy(codebook.at[pl.ds(start, share)], codes, sem)


def refresh_kernel(
    scale, code_potential, potential, codebook, tokens,
    out, held, codes, column, panel, sems, own_sem,
):
    own = own_code_copy(codebook, codes, own_sem)
    copies = chunk_copies(tokens, held, sems)
    own.start()
    for copy in copies[:AHEAD]:
        copy.start()
    halves, tiles = potential.shape[1], codes.shape[0] // LANES
    for h in range(tiles):
        row = code_potential[pl.ds(lax.axis_index("tok") * tiles + h, 1), :]
        column[pl.ds(h * LANES, LANES), :] = as_column(row) + scale
    own.wait()

    def chunk_scores(k):
        copies[k].wait()
        if k + AHEAD < len(copies):
            copies[k + AHEAD].start()
        part = pl.ds(k * CHUNK, CHUNK)
        panel[:, part] = (
            lax.dot_general(
                codes[...],
                held[part, :],
                (((1,), (1,)), ((), ())),
                preferred_element_type=jnp.float32,
            )
            * score_scale
        )

    assigned = jnp.zeros(out.shape, jnp.float32)
    chunk_scores(0)
    for k in range(len(copies)):
        if k + 1 < len(copies):
            chunk_scores(k + 1)
        for start in range(k * CHUNK, (k + 1) * CHUNK, DOT_CHUNK):
            weights = []
            for j in range(start // LANES, (start + DOT_CHUNK) // LANES):
                row = potential[j // halves, pl.ds(j % halves, 1), :]
                weights.append(
                    jnp.exp2(panel[:, tile(j)] + column[...] + row).astype(held.dtype)
                )
            assigned += jnp.dot(
                jnp.concatenate(weights, axis=1),
                held[pl.ds(start, DOT_CHUNK), :],
                preferred_element_type=jnp.float32,
            )
    mixed = codes[...].astype(jnp.float32) + assigned
    out[...] = mixed * lax.rsqrt(
        jnp.mean(mixed * mixed, axis=1, keepdims=True) + rms_epsilon
    )


def in_vmem(array):
    return pltpu.with_memory_space_constraint(array, pltpu.VMEM)


def in_hbm(array):
    return pltpu.with_memory_space_constraint(array, pltpu.HBM)


def call(kernel, out_shape, scratch=(), specs=None, out_specs=None, limit=24, elements=0, flops=0):
    vmem = pl.BlockSpec(memory_space=pltpu.VMEM)
    return pl.pallas_call(
        kernel,
        out_shape=out_shape,
        in_specs=specs,
        out_specs=out_specs if out_specs is not None else jax.tree.map(lambda _: vmem, out_shape),
        scratch_shapes=list(scratch),
        compiler_params=pltpu.CompilerParams(vmem_limit_bytes=limit * MIB),
        cost_estimate=pl.CostEstimate(
            flops=flops + 4 * elements, transcendentals=elements, bytes_accessed=4 * elements
        ),
    )


def per_device(tokens, codebook):
    tok_size, code_size = lax.axis_size("tok"), lax.axis_size("code")
    tok_rows, depth = tokens.shape
    code_rows = codebook.shape[0]
    total_tokens = tok_rows * tok_size
    total_codes = code_rows * code_size
    share = code_rows // tok_size
    row_tiles, code_tiles = tok_rows // LANES, code_rows // LANES
    elements = tok_rows * code_rows
    f32 = jnp.float32
    vmem = pl.BlockSpec(memory_space=pltpu.VMEM)
    hbm = pl.BlockSpec(memory_space=pltpu.HBM)
    to_tok = jax.ShapeDtypeStruct((tok_size, code_tiles, LANES), f32)
    to_code = jax.ShapeDtypeStruct((code_size, row_tiles, LANES), f32)
    column = pltpu.VMEM((tok_rows, LANES), f32)

    def exchange(copies, axis):
        return lax.all_to_all(copies, axis, 0, 0)

    scores, copies = call(
        scores_kernel,
        (pltpu.VMEM((tok_rows, code_rows), f32), to_tok),
        [
            pltpu.VMEM((code_rows, depth), codebook.dtype),
            pltpu.VMEM((tok_rows, depth), tokens.dtype),
            pltpu.VMEM((code_tiles, LANES), f32),
            pltpu.SemaphoreType.DMA((code_rows // CHUNK,)),
            pltpu.SemaphoreType.DMA,
        ],
        specs=[hbm, hbm],
        elements=elements,
        flops=2 * elements * depth,
    )(in_hbm(tokens), in_hbm(codebook))
    copies, own_tokens = lax.optimization_barrier((copies, tokens))
    all_tokens = lax.all_gather(own_tokens, "tok", axis=0, tiled=True)
    for step in range(ITERS):
        last = step == ITERS - 1
        potential = pltpu.VMEM((code_tiles, LANES), f32)
        copies, *code_potential = call(
            functools.partial(rows_kernel, math.log2(total_codes)),
            (to_code, potential) if last else (to_code,),
            [] if last else [potential],
            specs=[vmem, vmem],
            elements=elements,
        )(exchange(copies, "tok"), in_vmem(scores))
        received = exchange(copies, "code")
        if not last:
            copies = call(
                functools.partial(columns_kernel, math.log2(total_tokens)),
                to_tok,
                [column, potential],
                specs=[vmem, vmem],
                elements=elements,
            )(received, in_vmem(scores))
    (code_potential,) = code_potential

    copies = call(
        functools.partial(token_potential_kernel, math.log2(total_tokens)),
        jax.ShapeDtypeStruct((tok_size, row_tiles, LANES), f32),
        specs=[vmem],
    )(received)
    all_potential = exchange(copies, "tok")
    code_sems = pltpu.SemaphoreType.DMA((code_rows // CHUNK,))
    targets = call(
        functools.partial(targets_kernel, math.log2(total_tokens)),
        jax.ShapeDtypeStruct((tok_rows, code_rows), jnp.bfloat16),
        [
            column,
            pltpu.VMEM((tok_rows, code_rows), f32),
            pltpu.VMEM((tok_rows, code_rows), jnp.bfloat16),
            code_sems,
            code_sems,
        ],
        specs=[vmem, vmem, hbm],
        out_specs=hbm,
        elements=elements,
    )(copies, code_potential, in_hbm(scores))
    updated_codebook = call(
        functools.partial(refresh_kernel, math.log2(total_tokens)),
        jax.ShapeDtypeStruct((share, depth), f32),
        [
            pltpu.VMEM((total_tokens, depth), tokens.dtype),
            pltpu.VMEM((share, depth), codebook.dtype),
            pltpu.VMEM((share, LANES), f32),
            pltpu.VMEM((share, total_tokens), f32),
            pltpu.SemaphoreType.DMA((total_tokens // CHUNK,)),
            pltpu.SemaphoreType.DMA,
        ],
        specs=[vmem, vmem, hbm, hbm],
        elements=elements,
        flops=4 * elements * depth,
    )(code_potential, all_potential, in_hbm(codebook), in_hbm(all_tokens))
    return (targets, updated_codebook)


def solution(mesh):
    return jax.shard_map(
        per_device,
        mesh=mesh,
        in_specs=(P("tok", None), P("code", None)),
        out_specs=(P("tok", "code"), P(("code", "tok"), None)),
        check_vma=False,
    )
```

```python
import functools
import math

import jax
import jax.numpy as jnp
from jax import lax
from jax.experimental import pallas as pl
from jax.experimental.pallas import tpu as pltpu
from jax.sharding import PartitionSpec as P

ITERS = 3


sharpness_factor = 2.5
rms_epsilon = 1e-06

LANES = 128
CHUNK = 1024
DOT_CHUNK = 512
AHEAD = 2
MIB = 1 << 20

score_scale = sharpness_factor * math.log2(math.e)


def lse2(values, axis):
    top = jnp.max(values, axis=axis, keepdims=True)
    total = jnp.sum(jnp.exp2(values - top), axis=axis)
    return jnp.squeeze(top, axis) + jnp.log2(total)


def as_column(row):
    return jnp.broadcast_to(row, (LANES, LANES)).T


def tile(k):
    return pl.ds(pl.multiple_of(k * LANES, LANES), LANES)


def column_lse(scores, potential, k):
    values = scores[:, tile(k)]
    if potential is not None:
        values = values + potential[...]
    values = values.reshape(values.shape[0] // 8, 8, LANES)
    top = jnp.max(values, axis=0)
    total = jnp.sum(jnp.exp2(values - top[None]), axis=0)
    most = jnp.max(top, axis=0, keepdims=True)
    total = jnp.sum(total * jnp.exp2(top - most), axis=0, keepdims=True)
    return most + jnp.log2(total)


def send_copies(local, out):
    for d in range(out.shape[0]):
        out[d] = local[...]


def chunk_copies(source, held, sems, axis=0):
    copies = []
    for k in range(source.shape[axis] // CHUNK):
        part = (slice(None),) * axis + (pl.ds(k * CHUNK, CHUNK),)
        copies.append(pltpu.make_async_copy(source.at[part], held.at[part], sems.at[k]))
    return copies


def scores_kernel(tokens, codebook, scores, out, held, rows, local, sems, rows_sem):
    copies = chunk_copies(codebook, held, sems)
    rows_copy = pltpu.make_async_copy(tokens, rows, rows_sem)
    rows_copy.start()
    for copy in copies[:AHEAD]:
        copy.start()
    rows_copy.wait()
    for k in range(len(copies) + 1):
        if k < len(copies):
            copies[k].wait()
            if k + AHEAD < len(copies):
                copies[k + AHEAD].start()
            scores[:, pl.ds(k * CHUNK, CHUNK)] = (
                lax.dot_general(
                    rows[...],
                    held[pl.ds(k * CHUNK, CHUNK), :],
                    (((1,), (1,)), ((), ())),
                    preferred_element_type=jnp.float32,
                )
                * score_scale
            )
        if k > 0:
            for j in range((k - 1) * CHUNK // LANES, k * CHUNK // LANES):
                local[pl.ds(j, 1), :] = column_lse(scores, None, j)
    send_copies(local, out)


def columns_kernel(shift, received, scores, out, column, local):
    potential = -shift - lse2(received[...], 0)
    for h in range(potential.shape[0]):
        column[pl.ds(h * LANES, LANES), :] = as_column(potential[h : h + 1, :])

    def step(k, carry):
        local[pl.ds(k, 1), :] = column_lse(scores, column, k)
        return carry

    lax.fori_loop(0, local.shape[0], step, 0, unroll=8)
    send_copies(local, out)


def rows_kernel(shift, received, scores, out, potential):
    potential[...] = -shift - lse2(received[...], 0)
    tiles = potential.shape[0]
    partials = []
    for h in range(out.shape[1]):
        rows = pl.ds(h * LANES, LANES)

        def values(k):
            return scores[rows, tile(k)] + potential[pl.ds(k, 1), :]

        top = lax.fori_loop(
            0, tiles, lambda k, top: jnp.maximum(top, values(k)), values(0), unroll=8
        )
        total = lax.fori_loop(
            0,
            tiles,
            lambda k, total: total + jnp.exp2(values(k) - top),
            jnp.zeros((LANES, LANES), jnp.float32),
            unroll=8,
        )
        partials.append((top, total))
    lane = lax.broadcasted_iota(jnp.int32, (LANES, LANES), 1)
    local = jnp.zeros((LANES, LANES), jnp.float32)
    for h, (top, total) in enumerate(partials):
        most = jnp.max(top, axis=1, keepdims=True)
        total = jnp.sum(total * jnp.exp2(top - most), axis=1, keepdims=True)
        local = jnp.where(lane == h, most + jnp.log2(total), local)
    local = local.T[: out.shape[1], :]
    for d in range(out.shape[0]):
        out[d] = local


def token_potential_kernel(shift, received, out):
    potential = -shift - lse2(received[...], 0)
    for d in range(out.shape[0]):
        out[d] = potential


def targets_kernel(
    scale, token_potential, code_potential, scores, out, column, panel, held, sems, out_sems
):
    copies = chunk_copies(scores, panel, sems, 1)
    for copy in copies:
        copy.start()
    for h in range(token_potential.shape[1]):
        column[pl.ds(h * LANES, LANES), :] = as_column(token_potential[0, pl.ds(h, 1), :]) + scale
    out_copies = chunk_copies(held, out, out_sems, 1)
    for k in range(len(copies)):
        copies[k].wait()
        for j in range(k * CHUNK // LANES, (k + 1) * CHUNK // LANES):
            held[:, tile(j)] = jnp.exp2(
                panel[:, tile(j)] + column[...] + code_potential[pl.ds(j, 1), :]
            ).astype(held.dtype)
        out_copies[k].start()
    for copy in out_copies:
        copy.wait()


def own_code_copy(codebook, codes, sem):
    share = codes.shape[0]
    start = pl.multiple_of(lax.axis_index("tok") * share, share)
    return pltpu.make_async_copy(codebook.at[pl.ds(start, share)], codes, sem)


def refresh_kernel(
    scale, code_potential, potential, codebook, tokens,
    out, held, codes, column, panel, sems, own_sem,
):
    own = own_code_copy(codebook, codes, own_sem)
    copies = chunk_copies(tokens, held, sems)
    own.start()
    for copy in copies[:AHEAD]:
        copy.start()
    halves, tiles = potential.shape[1], codes.shape[0] // LANES
    for h in range(tiles):
        row = code_potential[pl.ds(lax.axis_index("tok") * tiles + h, 1), :]
        column[pl.ds(h * LANES, LANES), :] = as_column(row) + scale
    own.wait()

    def chunk_scores(k):
        copies[k].wait()
        if k + AHEAD < len(copies):
            copies[k + AHEAD].start()
        part = pl.ds(k * CHUNK, CHUNK)
        panel[:, part] = (
            lax.dot_general(
                codes[...],
                held[part, :],
                (((1,), (1,)), ((), ())),
                preferred_element_type=jnp.float32,
            )
            * score_scale
        )

    assigned = jnp.zeros(out.shape, jnp.float32)
    chunk_scores(0)
    for k in range(len(copies)):
        if k + 1 < len(copies):
            chunk_scores(k + 1)
        for start in range(k * CHUNK, (k + 1) * CHUNK, DOT_CHUNK):
            weights = []
            for j in range(start // LANES, (start + DOT_CHUNK) // LANES):
                row = potential[j // halves, pl.ds(j % halves, 1), :]
                weights.append(
                    jnp.exp2(panel[:, tile(j)] + column[...] + row).astype(held.dtype)
                )
            assigned += jnp.dot(
                jnp.concatenate(weights, axis=1),
                held[pl.ds(start, DOT_CHUNK), :],
                preferred_element_type=jnp.float32,
            )
    mixed = codes[...].astype(jnp.float32) + assigned
    out[...] = mixed * lax.rsqrt(
        jnp.mean(mixed * mixed, axis=1, keepdims=True) + rms_epsilon
    )


def in_vmem(array):
    return pltpu.with_memory_space_constraint(array, pltpu.VMEM)


def in_hbm(array):
    return pltpu.with_memory_space_constraint(array, pltpu.HBM)


def call(kernel, out_shape, scratch=(), specs=None, out_specs=None, limit=24, elements=0, flops=0):
    vmem = pl.BlockSpec(memory_space=pltpu.VMEM)
    return pl.pallas_call(
        kernel,
        out_shape=out_shape,
        in_specs=specs,
        out_specs=out_specs if out_specs is not None else jax.tree.map(lambda _: vmem, out_shape),
        scratch_shapes=list(scratch),
        compiler_params=pltpu.CompilerParams(vmem_limit_bytes=limit * MIB),
        cost_estimate=pl.CostEstimate(
            flops=flops + 4 * elements, transcendentals=elements, bytes_accessed=4 * elements
        ),
    )


def per_device(tokens, codebook):
    tok_size, code_size = lax.axis_size("tok"), lax.axis_size("code")
    tok_rows, depth = tokens.shape
    code_rows = codebook.shape[0]
    total_tokens = tok_rows * tok_size
    total_codes = code_rows * code_size
    share = code_rows // tok_size
    row_tiles, code_tiles = tok_rows // LANES, code_rows // LANES
    elements = tok_rows * code_rows
    f32 = jnp.float32
    vmem = pl.BlockSpec(memory_space=pltpu.VMEM)
    hbm = pl.BlockSpec(memory_space=pltpu.HBM)
    to_tok = jax.ShapeDtypeStruct((tok_size, code_tiles, LANES), f32)
    to_code = jax.ShapeDtypeStruct((code_size, row_tiles, LANES), f32)
    column = pltpu.VMEM((tok_rows, LANES), f32)

    def exchange(copies, axis):
        return lax.all_to_all(copies, axis, 0, 0)

    all_tokens = lax.all_gather(tokens, "tok", axis=0, tiled=True)

    scores, copies = call(
        scores_kernel,
        (pltpu.VMEM((tok_rows, code_rows), f32), to_tok),
        [
            pltpu.VMEM((code_rows, depth), codebook.dtype),
            pltpu.VMEM((tok_rows, depth), tokens.dtype),
            pltpu.VMEM((code_tiles, LANES), f32),
            pltpu.SemaphoreType.DMA((code_rows // CHUNK,)),
            pltpu.SemaphoreType.DMA,
        ],
        specs=[hbm, hbm],
        elements=elements,
        flops=2 * elements * depth,
    )(in_hbm(tokens), in_hbm(codebook))
    for step in range(ITERS):
        last = step == ITERS - 1
        potential = pltpu.VMEM((code_tiles, LANES), f32)
        copies, *code_potential = call(
            functools.partial(rows_kernel, math.log2(total_codes)),
            (to_code, potential) if last else (to_code,),
            [] if last else [potential],
            specs=[vmem, vmem],
            elements=elements,
        )(exchange(copies, "tok"), in_vmem(scores))
        received = exchange(copies, "code")
        if not last:
            copies = call(
                functools.partial(columns_kernel, math.log2(total_tokens)),
                to_tok,
                [column, potential],
                specs=[vmem, vmem],
                elements=elements,
            )(received, in_vmem(scores))
    (code_potential,) = code_potential

    copies = call(
        functools.partial(token_potential_kernel, math.log2(total_tokens)),
        jax.ShapeDtypeStruct((tok_size, row_tiles, LANES), f32),
        specs=[vmem],
    )(received)
    all_potential = exchange(copies, "tok")
    code_sems = pltpu.SemaphoreType.DMA((code_rows // CHUNK,))
    targets = call(
        functools.partial(targets_kernel, math.log2(total_tokens)),
        jax.ShapeDtypeStruct((tok_rows, code_rows), jnp.bfloat16),
        [
            column,
            pltpu.VMEM((tok_rows, code_rows), f32),
            pltpu.VMEM((tok_rows, code_rows), jnp.bfloat16),
            code_sems,
            code_sems,
        ],
        specs=[vmem, vmem, hbm],
        out_specs=hbm,
        elements=elements,
    )(copies, code_potential, in_hbm(scores))
    updated_codebook = call(
        functools.partial(refresh_kernel, math.log2(total_tokens)),
        jax.ShapeDtypeStruct((share, depth), f32),
        [
            pltpu.VMEM((total_tokens, depth), tokens.dtype),
            pltpu.VMEM((share, depth), codebook.dtype),
            pltpu.VMEM((share, LANES), f32),
            pltpu.VMEM((share, total_tokens), f32),
            pltpu.SemaphoreType.DMA((total_tokens // CHUNK,)),
            pltpu.SemaphoreType.DMA,
        ],
        specs=[vmem, vmem, hbm, hbm],
        elements=elements,
        flops=4 * elements * depth,
    )(code_potential, all_potential, in_hbm(codebook), in_hbm(all_tokens))
    return (targets, updated_codebook)


def solution(mesh):
    return jax.shard_map(
        per_device,
        mesh=mesh,
        in_specs=(P("tok", None), P("code", None)),
        out_specs=(P("tok", "code"), P(("code", "tok"), None)),
        check_vma=False,
    )
```

```python
import functools
import math

import jax
import jax.numpy as jnp
from jax import lax
from jax.experimental import pallas as pl
from jax.experimental.pallas import tpu as pltpu
from jax.sharding import PartitionSpec as P

ITERS = 3


sharpness_factor = 2.5
rms_epsilon = 1e-06

LANES = 128
CHUNKS = 5
DOT_CHUNK = 512
AHEAD = 2
MIB = 1 << 20

score_scale = sharpness_factor * math.log2(math.e)


def lse2(values, axis):
    top = jnp.max(values, axis=axis, keepdims=True)
    total = jnp.sum(jnp.exp2(values - top), axis=axis)
    return jnp.squeeze(top, axis) + jnp.log2(total)


def as_column(row):
    return jnp.broadcast_to(row, (LANES, LANES)).T


def tile(k):
    return pl.ds(pl.multiple_of(k * LANES, LANES), LANES)


def column_lse(scores, potential, k):
    values = scores[:, tile(k)]
    if potential is not None:
        values = values + potential[...]
    values = values.reshape(values.shape[0] // 8, 8, LANES)
    top = jnp.max(values, axis=0)
    total = jnp.sum(jnp.exp2(values - top[None]), axis=0)
    most = jnp.max(top, axis=0, keepdims=True)
    total = jnp.sum(total * jnp.exp2(top - most), axis=0, keepdims=True)
    return most + jnp.log2(total)


def send_copies(local, out):
    for d in range(out.shape[0]):
        out[d] = local[...]


def chunks(size):
    ends = [size // 8 * k for k in (0, 1, 3, 5, 7, 8)]
    return [(start, end - start) for start, end in zip(ends, ends[1:])]


def chunk_copies(source, held, sems, axis=0):
    copies = []
    for k, (start, length) in enumerate(chunks(source.shape[axis])):
        part = (slice(None),) * axis + (pl.ds(start, length),)
        copies.append(pltpu.make_async_copy(source.at[part], held.at[part], sems.at[k]))
    return copies


def tiles_of(start, length):
    return range(start // LANES, (start + length) // LANES)


def scores_kernel(tokens, codebook, scores, out, held, rows, local, sems, rows_sem):
    copies = chunk_copies(codebook, held, sems)
    rows_copy = pltpu.make_async_copy(tokens, rows, rows_sem)
    rows_copy.start()
    for copy in copies[:AHEAD]:
        copy.start()
    rows_copy.wait()
    parts = chunks(codebook.shape[0])
    for k in range(len(parts) + 1):
        if k < len(parts):
            copies[k].wait()
            if k + AHEAD < len(parts):
                copies[k + AHEAD].start()
            part = pl.ds(*parts[k])
            scores[:, part] = (
                lax.dot_general(
                    rows[...],
                    held[part, :],
                    (((1,), (1,)), ((), ())),
                    preferred_element_type=jnp.float32,
                )
                * score_scale
            )
        if k > 0:
            for j in tiles_of(*parts[k - 1]):
                local[pl.ds(j, 1), :] = column_lse(scores, None, j)
    send_copies(local, out)


def columns_kernel(shift, received, scores, out, column, local):
    potential = -shift - lse2(received[...], 0)
    for h in range(potential.shape[0]):
        column[pl.ds(h * LANES, LANES), :] = as_column(potential[h : h + 1, :])

    def step(k, carry):
        local[pl.ds(k, 1), :] = column_lse(scores, column, k)
        return carry

    lax.fori_loop(0, local.shape[0], step, 0, unroll=8)
    send_copies(local, out)


def rows_kernel(shift, received, scores, out, potential):
    potential[...] = -shift - lse2(received[...], 0)
    tiles = potential.shape[0]
    partials = []
    for h in range(out.shape[1]):
        rows = pl.ds(h * LANES, LANES)

        def values(k):
            return scores[rows, tile(k)] + potential[pl.ds(k, 1), :]

        top = lax.fori_loop(
            0, tiles, lambda k, top: jnp.maximum(top, values(k)), values(0), unroll=8
        )
        total = lax.fori_loop(
            0,
            tiles,
            lambda k, total: total + jnp.exp2(values(k) - top),
            jnp.zeros((LANES, LANES), jnp.float32),
            unroll=8,
        )
        partials.append((top, total))
    for h, (top, total) in enumerate(partials):
        top = top.T
        most = jnp.max(top, axis=0, keepdims=True)
        total = jnp.sum(total.T * jnp.exp2(top - most), axis=0, keepdims=True)
        local = most + jnp.log2(total)
        for d in range(out.shape[0]):
            out[d, pl.ds(h, 1), :] = local


def token_potential_kernel(shift, received, out):
    potential = -shift - lse2(received[...], 0)
    for d in range(out.shape[0]):
        out[d] = potential


def targets_kernel(
    scale, token_potential, code_potential, scores, out, column, panel, held, sems, out_sems
):
    copies = chunk_copies(scores, panel, sems, 1)
    for copy in copies:
        copy.start()
    for h in range(token_potential.shape[1]):
        column[pl.ds(h * LANES, LANES), :] = as_column(token_potential[0, pl.ds(h, 1), :]) + scale
    out_copies = chunk_copies(held, out, out_sems, 1)
    for k, part in enumerate(chunks(scores.shape[1])):
        copies[k].wait()
        for j in tiles_of(*part):
            held[:, tile(j)] = jnp.exp2(
                panel[:, tile(j)] + column[...] + code_potential[pl.ds(j, 1), :]
            ).astype(held.dtype)
        out_copies[k].start()
    for copy in out_copies:
        copy.wait()


def own_code_copy(codebook, codes, sem):
    share = codes.shape[0]
    start = pl.multiple_of(lax.axis_index("tok") * share, share)
    return pltpu.make_async_copy(codebook.at[pl.ds(start, share)], codes, sem)


def refresh_kernel(
    scale, code_potential, potential, codebook, tokens,
    out, held, codes, column, panel, sems, own_sem,
):
    own = own_code_copy(codebook, codes, own_sem)
    copies = chunk_copies(tokens, held, sems)
    own.start()
    for copy in copies[:AHEAD]:
        copy.start()
    halves, tiles = potential.shape[1], codes.shape[0] // LANES
    for h in range(tiles):
        row = code_potential[pl.ds(lax.axis_index("tok") * tiles + h, 1), :]
        column[pl.ds(h * LANES, LANES), :] = as_column(row) + scale
    own.wait()

    parts = chunks(tokens.shape[0])

    def chunk_scores(k):
        copies[k].wait()
        if k + AHEAD < len(copies):
            copies[k + AHEAD].start()
        part = pl.ds(*parts[k])
        panel[:, part] = (
            lax.dot_general(
                codes[...],
                held[part, :],
                (((1,), (1,)), ((), ())),
                preferred_element_type=jnp.float32,
            )
            * score_scale
        )

    assigned = jnp.zeros(out.shape, jnp.float32)
    chunk_scores(0)
    for k, (first, length) in enumerate(parts):
        if k + 1 < len(parts):
            chunk_scores(k + 1)
        for start in range(first, first + length, DOT_CHUNK):
            weights = []
            for j in tiles_of(start, DOT_CHUNK):
                row = potential[j // halves, pl.ds(j % halves, 1), :]
                weights.append(
                    jnp.exp2(panel[:, tile(j)] + column[...] + row).astype(held.dtype)
                )
            assigned += jnp.dot(
                jnp.concatenate(weights, axis=1),
                held[pl.ds(start, DOT_CHUNK), :],
                preferred_element_type=jnp.float32,
            )
    mixed = codes[...].astype(jnp.float32) + assigned
    out[...] = mixed * lax.rsqrt(
        jnp.mean(mixed * mixed, axis=1, keepdims=True) + rms_epsilon
    )


def in_vmem(array):
    return pltpu.with_memory_space_constraint(array, pltpu.VMEM)


def in_hbm(array):
    return pltpu.with_memory_space_constraint(array, pltpu.HBM)


def call(kernel, out_shape, scratch=(), specs=None, out_specs=None, limit=24, elements=0, flops=0):
    vmem = pl.BlockSpec(memory_space=pltpu.VMEM)
    return pl.pallas_call(
        kernel,
        out_shape=out_shape,
        in_specs=specs,
        out_specs=out_specs if out_specs is not None else jax.tree.map(lambda _: vmem, out_shape),
        scratch_shapes=list(scratch),
        compiler_params=pltpu.CompilerParams(vmem_limit_bytes=limit * MIB),
        cost_estimate=pl.CostEstimate(
            flops=flops + 4 * elements, transcendentals=elements, bytes_accessed=4 * elements
        ),
    )


def per_device(tokens, codebook):
    tok_size, code_size = lax.axis_size("tok"), lax.axis_size("code")
    tok_rows, depth = tokens.shape
    code_rows = codebook.shape[0]
    total_tokens = tok_rows * tok_size
    total_codes = code_rows * code_size
    share = code_rows // tok_size
    row_tiles, code_tiles = tok_rows // LANES, code_rows // LANES
    elements = tok_rows * code_rows
    f32 = jnp.float32
    vmem = pl.BlockSpec(memory_space=pltpu.VMEM)
    hbm = pl.BlockSpec(memory_space=pltpu.HBM)
    to_tok = jax.ShapeDtypeStruct((tok_size, code_tiles, LANES), f32)
    to_code = jax.ShapeDtypeStruct((code_size, row_tiles, LANES), f32)
    column = pltpu.VMEM((tok_rows, LANES), f32)

    def exchange(copies, axis):
        return lax.all_to_all(copies, axis, 0, 0)

    all_tokens = lax.all_gather(tokens, "tok", axis=0, tiled=True)

    scores, copies = call(
        scores_kernel,
        (pltpu.VMEM((tok_rows, code_rows), f32), to_tok),
        [
            pltpu.VMEM((code_rows, depth), codebook.dtype),
            pltpu.VMEM((tok_rows, depth), tokens.dtype),
            pltpu.VMEM((code_tiles, LANES), f32),
            pltpu.SemaphoreType.DMA((CHUNKS,)),
            pltpu.SemaphoreType.DMA,
        ],
        specs=[hbm, hbm],
        elements=elements,
        flops=2 * elements * depth,
    )(in_hbm(tokens), in_hbm(codebook))
    for step in range(ITERS):
        last = step == ITERS - 1
        potential = pltpu.VMEM((code_tiles, LANES), f32)
        copies, *code_potential = call(
            functools.partial(rows_kernel, math.log2(total_codes)),
            (to_code, potential) if last else (to_code,),
            [] if last else [potential],
            specs=[vmem, vmem],
            elements=elements,
        )(exchange(copies, "tok"), in_vmem(scores))
        received = exchange(copies, "code")
        if not last:
            copies = call(
                functools.partial(columns_kernel, math.log2(total_tokens)),
                to_tok,
                [column, potential],
                specs=[vmem, vmem],
                elements=elements,
            )(received, in_vmem(scores))
    (code_potential,) = code_potential

    copies = call(
        functools.partial(token_potential_kernel, math.log2(total_tokens)),
        jax.ShapeDtypeStruct((tok_size, row_tiles, LANES), f32),
        specs=[vmem],
    )(received)
    all_potential = exchange(copies, "tok")
    code_sems = pltpu.SemaphoreType.DMA((CHUNKS,))
    targets = call(
        functools.partial(targets_kernel, math.log2(total_tokens)),
        jax.ShapeDtypeStruct((tok_rows, code_rows), jnp.bfloat16),
        [
            column,
            pltpu.VMEM((tok_rows, code_rows), f32),
            pltpu.VMEM((tok_rows, code_rows), jnp.bfloat16),
            code_sems,
            code_sems,
        ],
        specs=[vmem, vmem, hbm],
        out_specs=hbm,
        elements=elements,
    )(copies, code_potential, in_hbm(scores))
    updated_codebook = call(
        functools.partial(refresh_kernel, math.log2(total_tokens)),
        jax.ShapeDtypeStruct((share, depth), f32),
        [
            pltpu.VMEM((total_tokens, depth), tokens.dtype),
            pltpu.VMEM((share, depth), codebook.dtype),
            pltpu.VMEM((share, LANES), f32),
            pltpu.VMEM((share, total_tokens), f32),
            pltpu.SemaphoreType.DMA((CHUNKS,)),
            pltpu.SemaphoreType.DMA,
        ],
        specs=[vmem, vmem, hbm, hbm],
        elements=elements,
        flops=4 * elements * depth,
    )(code_potential, all_potential, in_hbm(codebook), in_hbm(all_tokens))
    return (targets, updated_codebook)


def solution(mesh):
    return jax.shard_map(
        per_device,
        mesh=mesh,
        in_specs=(P("tok", None), P("code", None)),
        out_specs=(P("tok", "code"), P(("code", "tok"), None)),
        check_vma=False,
    )
```

```python
import functools
import math

import jax
import jax.numpy as jnp
from jax import lax
from jax.experimental import pallas as pl
from jax.experimental.pallas import tpu as pltpu
from jax.sharding import PartitionSpec as P

ITERS = 3


sharpness_factor = 2.5
rms_epsilon = 1e-06

LANES = 128
CHUNK = 1024
DOT_CHUNK = 512
AHEAD = 2
MIB = 1 << 20

score_scale = sharpness_factor * math.log2(math.e)


def lse2(values, axis):
    top = jnp.max(values, axis=axis, keepdims=True)
    total = jnp.sum(jnp.exp2(values - top), axis=axis)
    return jnp.squeeze(top, axis) + jnp.log2(total)


def as_column(row):
    return jnp.broadcast_to(row, (LANES, LANES)).T


def tile(k):
    return pl.ds(pl.multiple_of(k * LANES, LANES), LANES)


def column_lse(scores, potential, k):
    values = scores[:, tile(k)]
    if potential is not None:
        values = values + potential[...]
    values = values.reshape(values.shape[0] // 8, 8, LANES)
    top = jnp.max(values, axis=0)
    total = jnp.sum(jnp.exp2(values - top[None]), axis=0)
    most = jnp.max(top, axis=0, keepdims=True)
    total = jnp.sum(total * jnp.exp2(top - most), axis=0, keepdims=True)
    return most + jnp.log2(total)


def send_copies(local, out):
    for d in range(out.shape[0]):
        out[d] = local[...]


def chunk_copies(source, held, sems, axis=0):
    copies = []
    for k in range(source.shape[axis] // CHUNK):
        part = (slice(None),) * axis + (pl.ds(k * CHUNK, CHUNK),)
        copies.append(pltpu.make_async_copy(source.at[part], held.at[part], sems.at[k]))
    return copies


def scores_kernel(tokens, codebook, scores, out, held, rows, local, sems, rows_sem):
    copies = chunk_copies(codebook, held, sems)
    rows_copy = pltpu.make_async_copy(tokens, rows, rows_sem)
    rows_copy.start()
    for copy in copies[:AHEAD]:
        copy.start()
    rows_copy.wait()
    for k in range(len(copies) + 1):
        if k < len(copies):
            copies[k].wait()
            if k + AHEAD < len(copies):
                copies[k + AHEAD].start()
            scores[:, pl.ds(k * CHUNK, CHUNK)] = (
                lax.dot_general(
                    rows[...],
                    held[pl.ds(k * CHUNK, CHUNK), :],
                    (((1,), (1,)), ((), ())),
                    preferred_element_type=jnp.float32,
                )
                * score_scale
            )
        if k > 0:
            for j in range((k - 1) * CHUNK // LANES, k * CHUNK // LANES):
                local[pl.ds(j, 1), :] = column_lse(scores, None, j)
    send_copies(local, out)


def columns_kernel(shift, received, scores, out, column, local):
    potential = -shift - lse2(received[...], 0)
    for h in range(potential.shape[0]):
        column[pl.ds(h * LANES, LANES), :] = as_column(potential[h : h + 1, :])

    def step(k, carry):
        local[pl.ds(k, 1), :] = column_lse(scores, column, k)
        return carry

    lax.fori_loop(0, local.shape[0], step, 0, unroll=8)
    send_copies(local, out)


def row_partials(scores, potential, shape):
    local = lse2(scores + potential.reshape(1, scores.shape[1]), 1)
    return jnp.broadcast_to(local.reshape(shape[1:]), shape)


def token_potential_kernel(shift, received, out):
    potential = -shift - lse2(received[...], 0)
    for d in range(out.shape[0]):
        out[d] = potential


def targets_kernel(
    scale, token_potential, code_potential, scores, out, column, panel, held, sems, out_sems
):
    copies = chunk_copies(scores, panel, sems, 1)
    for copy in copies:
        copy.start()
    for h in range(token_potential.shape[1]):
        column[pl.ds(h * LANES, LANES), :] = as_column(token_potential[0, pl.ds(h, 1), :]) + scale
    out_copies = chunk_copies(held, out, out_sems, 1)
    for k in range(len(copies)):
        copies[k].wait()
        for j in range(k * CHUNK // LANES, (k + 1) * CHUNK // LANES):
            held[:, tile(j)] = jnp.exp2(
                panel[:, tile(j)] + column[...] + code_potential[pl.ds(j, 1), :]
            ).astype(held.dtype)
        out_copies[k].start()
    for copy in out_copies:
        copy.wait()


def own_code_copy(codebook, codes, sem):
    share = codes.shape[0]
    start = pl.multiple_of(lax.axis_index("tok") * share, share)
    return pltpu.make_async_copy(codebook.at[pl.ds(start, share)], codes, sem)


def refresh_kernel(
    scale, code_potential, potential, codebook, tokens,
    out, held, codes, column, panel, sems, own_sem,
):
    own = own_code_copy(codebook, codes, own_sem)
    copies = chunk_copies(tokens, held, sems)
    own.start()
    for copy in copies[:AHEAD]:
        copy.start()
    halves, tiles = potential.shape[1], codes.shape[0] // LANES
    for h in range(tiles):
        row = code_potential[pl.ds(lax.axis_index("tok") * tiles + h, 1), :]
        column[pl.ds(h * LANES, LANES), :] = as_column(row) + scale
    own.wait()

    def chunk_scores(k):
        copies[k].wait()
        if k + AHEAD < len(copies):
            copies[k + AHEAD].start()
        part = pl.ds(k * CHUNK, CHUNK)
        panel[:, part] = (
            lax.dot_general(
                codes[...],
                held[part, :],
                (((1,), (1,)), ((), ())),
                preferred_element_type=jnp.float32,
            )
            * score_scale
        )

    assigned = jnp.zeros(out.shape, jnp.float32)
    chunk_scores(0)
    for k in range(len(copies)):
        if k + 1 < len(copies):
            chunk_scores(k + 1)
        for start in range(k * CHUNK, (k + 1) * CHUNK, DOT_CHUNK):
            weights = []
            for j in range(start // LANES, (start + DOT_CHUNK) // LANES):
                row = potential[j // halves, pl.ds(j % halves, 1), :]
                weights.append(
                    jnp.exp2(panel[:, tile(j)] + column[...] + row).astype(held.dtype)
                )
            assigned += jnp.dot(
                jnp.concatenate(weights, axis=1),
                held[pl.ds(start, DOT_CHUNK), :],
                preferred_element_type=jnp.float32,
            )
    mixed = codes[...].astype(jnp.float32) + assigned
    out[...] = mixed * lax.rsqrt(
        jnp.mean(mixed * mixed, axis=1, keepdims=True) + rms_epsilon
    )


def in_vmem(array):
    return pltpu.with_memory_space_constraint(array, pltpu.VMEM)


def in_hbm(array):
    return pltpu.with_memory_space_constraint(array, pltpu.HBM)


def call(kernel, out_shape, scratch=(), specs=None, out_specs=None, limit=24, elements=0, flops=0):
    vmem = pl.BlockSpec(memory_space=pltpu.VMEM)
    return pl.pallas_call(
        kernel,
        out_shape=out_shape,
        in_specs=specs,
        out_specs=out_specs if out_specs is not None else jax.tree.map(lambda _: vmem, out_shape),
        scratch_shapes=list(scratch),
        compiler_params=pltpu.CompilerParams(vmem_limit_bytes=limit * MIB),
        cost_estimate=pl.CostEstimate(
            flops=flops + 4 * elements, transcendentals=elements, bytes_accessed=4 * elements
        ),
    )


def per_device(tokens, codebook):
    tok_size, code_size = lax.axis_size("tok"), lax.axis_size("code")
    tok_rows, depth = tokens.shape
    code_rows = codebook.shape[0]
    total_tokens = tok_rows * tok_size
    total_codes = code_rows * code_size
    share = code_rows // tok_size
    row_tiles, code_tiles = tok_rows // LANES, code_rows // LANES
    elements = tok_rows * code_rows
    f32 = jnp.float32
    vmem = pl.BlockSpec(memory_space=pltpu.VMEM)
    hbm = pl.BlockSpec(memory_space=pltpu.HBM)
    to_tok = jax.ShapeDtypeStruct((tok_size, code_tiles, LANES), f32)
    to_code = (code_size, row_tiles, LANES)
    column = pltpu.VMEM((tok_rows, LANES), f32)

    def exchange(copies, axis):
        return lax.all_to_all(copies, axis, 0, 0)

    all_tokens = lax.all_gather(tokens, "tok", axis=0, tiled=True)

    scores, copies = call(
        scores_kernel,
        (pltpu.VMEM((tok_rows, code_rows), f32), to_tok),
        [
            pltpu.VMEM((code_rows, depth), codebook.dtype),
            pltpu.VMEM((tok_rows, depth), tokens.dtype),
            pltpu.VMEM((code_tiles, LANES), f32),
            pltpu.SemaphoreType.DMA((code_rows // CHUNK,)),
            pltpu.SemaphoreType.DMA,
        ],
        specs=[hbm, hbm],
        elements=elements,
        flops=2 * elements * depth,
    )(in_hbm(tokens), in_hbm(codebook))
    for step in range(ITERS):
        last = step == ITERS - 1
        potential = pltpu.VMEM((code_tiles, LANES), f32)
        code_potential = -math.log2(total_codes) - lse2(exchange(copies, "tok"), 0)
        copies = row_partials(scores, code_potential, to_code)
        received = exchange(copies, "code")
        if not last:
            copies = call(
                functools.partial(columns_kernel, math.log2(total_tokens)),
                to_tok,
                [column, potential],
                specs=[vmem, vmem],
                elements=elements,
            )(received, in_vmem(scores))
    copies = call(
        functools.partial(token_potential_kernel, math.log2(total_tokens)),
        jax.ShapeDtypeStruct((tok_size, row_tiles, LANES), f32),
        specs=[vmem],
    )(received)
    all_potential = exchange(copies, "tok")
    code_sems = pltpu.SemaphoreType.DMA((code_rows // CHUNK,))
    targets = call(
        functools.partial(targets_kernel, math.log2(total_tokens)),
        jax.ShapeDtypeStruct((tok_rows, code_rows), jnp.bfloat16),
        [
            column,
            pltpu.VMEM((tok_rows, code_rows), f32),
            pltpu.VMEM((tok_rows, code_rows), jnp.bfloat16),
            code_sems,
            code_sems,
        ],
        specs=[vmem, vmem, hbm],
        out_specs=hbm,
        elements=elements,
    )(copies, code_potential, in_hbm(scores))
    updated_codebook = call(
        functools.partial(refresh_kernel, math.log2(total_tokens)),
        jax.ShapeDtypeStruct((share, depth), f32),
        [
            pltpu.VMEM((total_tokens, depth), tokens.dtype),
            pltpu.VMEM((share, depth), codebook.dtype),
            pltpu.VMEM((share, LANES), f32),
            pltpu.VMEM((share, total_tokens), f32),
            pltpu.SemaphoreType.DMA((total_tokens // CHUNK,)),
            pltpu.SemaphoreType.DMA,
        ],
        specs=[vmem, vmem, hbm, hbm],
        elements=elements,
        flops=4 * elements * depth,
    )(code_potential, all_potential, in_hbm(codebook), in_hbm(all_tokens))
    return (targets, updated_codebook)


def solution(mesh):
    return jax.shard_map(
        per_device,
        mesh=mesh,
        in_specs=(P("tok", None), P("code", None)),
        out_specs=(P("tok", "code"), P(("code", "tok"), None)),
        check_vma=False,
    )
```

```python
import functools
import math

import jax
import jax.numpy as jnp
from jax import lax
from jax.experimental import pallas as pl
from jax.experimental.pallas import tpu as pltpu
from jax.sharding import PartitionSpec as P

ITERS = 3


sharpness_factor = 2.5
rms_epsilon = 1e-06

LANES = 128
CHUNK = 1024
DOT_CHUNK = 512
AHEAD = 2
CODE = ("z", "core")
MIB = 1 << 20

score_scale = sharpness_factor * math.log2(math.e)


def lse2(values, axis):
    top = jnp.max(values, axis=axis, keepdims=True)
    total = jnp.sum(jnp.exp2(values - top), axis=axis)
    return jnp.squeeze(top, axis) + jnp.log2(total)


def as_column(row):
    return jnp.broadcast_to(row, (LANES, LANES)).T


def tile(k):
    return pl.ds(pl.multiple_of(k * LANES, LANES), LANES)


def column_lse(scores, potential, k):
    values = scores[:, tile(k)]
    if potential is not None:
        values = values + potential[...]
    values = values.reshape(values.shape[0] // 8, 8, LANES)
    top = jnp.max(values, axis=0)
    total = jnp.sum(jnp.exp2(values - top[None]), axis=0)
    most = jnp.max(top, axis=0, keepdims=True)
    total = jnp.sum(total * jnp.exp2(top - most), axis=0, keepdims=True)
    return most + jnp.log2(total)


def send_copies(local, out):
    for d in range(out.shape[0]):
        out[d] = local[...]


def chunk_copies(source, held, sems, axis=0):
    copies = []
    for k in range(source.shape[axis] // CHUNK):
        part = (slice(None),) * axis + (pl.ds(k * CHUNK, CHUNK),)
        copies.append(pltpu.make_async_copy(source.at[part], held.at[part], sems.at[k]))
    return copies


def scores_kernel(tokens, codebook, scores, out, held, rows, local, sems, rows_sem):
    copies = chunk_copies(codebook, held, sems)
    rows_copy = pltpu.make_async_copy(tokens, rows, rows_sem)
    rows_copy.start()
    for copy in copies[:AHEAD]:
        copy.start()
    rows_copy.wait()
    for k in range(len(copies) + 1):
        if k < len(copies):
            copies[k].wait()
            if k + AHEAD < len(copies):
                copies[k + AHEAD].start()
            scores[:, pl.ds(k * CHUNK, CHUNK)] = (
                lax.dot_general(
                    rows[...],
                    held[pl.ds(k * CHUNK, CHUNK), :],
                    (((1,), (1,)), ((), ())),
                    preferred_element_type=jnp.float32,
                )
                * score_scale
            )
        if k > 0:
            for j in range((k - 1) * CHUNK // LANES, k * CHUNK // LANES):
                local[pl.ds(j, 1), :] = column_lse(scores, None, j)
    send_copies(local, out)


def columns_kernel(shift, received, scores, out, column, local):
    potential = -shift - lse2(received[...], 0)
    for h in range(potential.shape[0]):
        column[pl.ds(h * LANES, LANES), :] = as_column(potential[h : h + 1, :])

    def step(k, carry):
        local[pl.ds(k, 1), :] = column_lse(scores, column, k)
        return carry

    lax.fori_loop(0, local.shape[0], step, 0, unroll=8)
    send_copies(local, out)


def rows_kernel(shift, received, scores, out, potential):
    potential[...] = -shift - lse2(received[...], 0)
    tiles = potential.shape[0]
    partials = []
    for h in range(out.shape[1]):
        rows = pl.ds(h * LANES, LANES)

        def values(k):
            return scores[rows, tile(k)] + potential[pl.ds(k, 1), :]

        top = lax.fori_loop(
            0, tiles, lambda k, top: jnp.maximum(top, values(k)), values(0), unroll=8
        )
        total = lax.fori_loop(
            0,
            tiles,
            lambda k, total: total + jnp.exp2(values(k) - top),
            jnp.zeros((LANES, LANES), jnp.float32),
            unroll=8,
        )
        partials.append((top, total))
    for h, (top, total) in enumerate(partials):
        top = top.T
        most = jnp.max(top, axis=0, keepdims=True)
        total = jnp.sum(total.T * jnp.exp2(top - most), axis=0, keepdims=True)
        local = most + jnp.log2(total)
        for d in range(out.shape[0]):
            out[d, pl.ds(h, 1), :] = local


def token_potential_kernel(shift, received, out):
    potential = -shift - lse2(received[...], 0)
    for d in range(out.shape[0]):
        out[d] = potential


def targets_kernel(
    scale, token_potential, code_potential, scores, out, column, panel, held, sems, out_sems
):
    copies = chunk_copies(scores, panel, sems, 1)
    for copy in copies:
        copy.start()
    for h in range(token_potential.shape[1]):
        column[pl.ds(h * LANES, LANES), :] = as_column(token_potential[0, pl.ds(h, 1), :]) + scale
    out_copies = chunk_copies(held, out, out_sems, 1)
    for k in range(len(copies)):
        copies[k].wait()
        for j in range(k * CHUNK // LANES, (k + 1) * CHUNK // LANES):
            held[:, tile(j)] = jnp.exp2(
                panel[:, tile(j)] + column[...] + code_potential[pl.ds(j, 1), :]
            ).astype(held.dtype)
        out_copies[k].start()
    for copy in out_copies:
        copy.wait()


def own_code_copy(codebook, codes, sem):
    share = codes.shape[0]
    start = pl.multiple_of(lax.axis_index("tok") * share, share)
    return pltpu.make_async_copy(codebook.at[pl.ds(start, share)], codes, sem)


def refresh_kernel(
    scale, code_potential, potential, codebook, tokens,
    out, held, codes, column, panel, sems, own_sem,
):
    own = own_code_copy(codebook, codes, own_sem)
    copies = chunk_copies(tokens, held, sems)
    own.start()
    for copy in copies[:AHEAD]:
        copy.start()
    halves, tiles = potential.shape[1], codes.shape[0] // LANES
    for h in range(tiles):
        row = code_potential[pl.ds(lax.axis_index("tok") * tiles + h, 1), :]
        column[pl.ds(h * LANES, LANES), :] = as_column(row) + scale
    own.wait()

    def chunk_scores(k):
        copies[k].wait()
        if k + AHEAD < len(copies):
            copies[k + AHEAD].start()
        part = pl.ds(k * CHUNK, CHUNK)
        panel[:, part] = (
            lax.dot_general(
                codes[...],
                held[part, :],
                (((1,), (1,)), ((), ())),
                preferred_element_type=jnp.float32,
            )
            * score_scale
        )

    assigned = jnp.zeros(out.shape, jnp.float32)
    chunk_scores(0)
    for k in range(len(copies)):
        if k + 1 < len(copies):
            chunk_scores(k + 1)
        for start in range(k * CHUNK, (k + 1) * CHUNK, DOT_CHUNK):
            weights = []
            for j in range(start // LANES, (start + DOT_CHUNK) // LANES):
                row = potential[j // halves, pl.ds(j % halves, 1), :]
                weights.append(
                    jnp.exp2(panel[:, tile(j)] + column[...] + row).astype(held.dtype)
                )
            assigned += jnp.dot(
                jnp.concatenate(weights, axis=1),
                held[pl.ds(start, DOT_CHUNK), :],
                preferred_element_type=jnp.float32,
            )
    mixed = codes[...].astype(jnp.float32) + assigned
    out[...] = mixed * lax.rsqrt(
        jnp.mean(mixed * mixed, axis=1, keepdims=True) + rms_epsilon
    )


def in_vmem(array):
    return pltpu.with_memory_space_constraint(array, pltpu.VMEM)


def in_hbm(array):
    return pltpu.with_memory_space_constraint(array, pltpu.HBM)


def call(kernel, out_shape, scratch=(), specs=None, out_specs=None, limit=24, elements=0, flops=0):
    vmem = pl.BlockSpec(memory_space=pltpu.VMEM)
    return pl.pallas_call(
        kernel,
        out_shape=out_shape,
        in_specs=specs,
        out_specs=out_specs if out_specs is not None else jax.tree.map(lambda _: vmem, out_shape),
        scratch_shapes=list(scratch),
        compiler_params=pltpu.CompilerParams(vmem_limit_bytes=limit * MIB),
        cost_estimate=pl.CostEstimate(
            flops=flops + 4 * elements, transcendentals=elements, bytes_accessed=4 * elements
        ),
    )


def per_device(tokens, codebook):
    tok_size, code_size = lax.axis_size("tok"), lax.axis_size(CODE)
    tok_rows, depth = tokens.shape
    code_rows = codebook.shape[0]
    total_tokens = tok_rows * tok_size
    total_codes = code_rows * code_size
    share = code_rows // tok_size
    row_tiles, code_tiles = tok_rows // LANES, code_rows // LANES
    elements = tok_rows * code_rows
    f32 = jnp.float32
    vmem = pl.BlockSpec(memory_space=pltpu.VMEM)
    hbm = pl.BlockSpec(memory_space=pltpu.HBM)
    to_tok = jax.ShapeDtypeStruct((tok_size, code_tiles, LANES), f32)
    to_code = jax.ShapeDtypeStruct((code_size, row_tiles, LANES), f32)
    column = pltpu.VMEM((tok_rows, LANES), f32)

    def exchange(copies, axis):
        return lax.all_to_all(copies, axis, 0, 0)

    part_rows = tok_rows // lax.axis_size("core")
    own_part = lax.dynamic_slice_in_dim(
        tokens, lax.axis_index("core") * part_rows, part_rows, 0
    )
    all_tokens = lax.all_gather(own_part, ("tok", "core"), axis=0, tiled=True)

    scores, copies = call(
        scores_kernel,
        (pltpu.VMEM((tok_rows, code_rows), f32), to_tok),
        [
            pltpu.VMEM((code_rows, depth), codebook.dtype),
            pltpu.VMEM((tok_rows, depth), tokens.dtype),
            pltpu.VMEM((code_tiles, LANES), f32),
            pltpu.SemaphoreType.DMA((code_rows // CHUNK,)),
            pltpu.SemaphoreType.DMA,
        ],
        specs=[hbm, hbm],
        elements=elements,
        flops=2 * elements * depth,
    )(in_hbm(tokens), in_hbm(codebook))
    for step in range(ITERS):
        last = step == ITERS - 1
        potential = pltpu.VMEM((code_tiles, LANES), f32)
        copies, *code_potential = call(
            functools.partial(rows_kernel, math.log2(total_codes)),
            (to_code, potential) if last else (to_code,),
            [] if last else [potential],
            specs=[vmem, vmem],
            elements=elements,
        )(exchange(copies, "tok"), in_vmem(scores))
        received = exchange(copies, CODE)
        if not last:
            copies = call(
                functools.partial(columns_kernel, math.log2(total_tokens)),
                to_tok,
                [column, potential],
                specs=[vmem, vmem],
                elements=elements,
            )(received, in_vmem(scores))
    (code_potential,) = code_potential

    copies = call(
        functools.partial(token_potential_kernel, math.log2(total_tokens)),
        jax.ShapeDtypeStruct((tok_size, row_tiles, LANES), f32),
        specs=[vmem],
    )(received)
    all_potential = exchange(copies, "tok")
    code_sems = pltpu.SemaphoreType.DMA((code_rows // CHUNK,))
    targets = call(
        functools.partial(targets_kernel, math.log2(total_tokens)),
        jax.ShapeDtypeStruct((tok_rows, code_rows), jnp.bfloat16),
        [
            column,
            pltpu.VMEM((tok_rows, code_rows), f32),
            pltpu.VMEM((tok_rows, code_rows), jnp.bfloat16),
            code_sems,
            code_sems,
        ],
        specs=[vmem, vmem, hbm],
        out_specs=hbm,
        elements=elements,
    )(copies, code_potential, in_hbm(scores))
    updated_codebook = call(
        functools.partial(refresh_kernel, math.log2(total_tokens)),
        jax.ShapeDtypeStruct((share, depth), f32),
        [
            pltpu.VMEM((total_tokens, depth), tokens.dtype),
            pltpu.VMEM((share, depth), codebook.dtype),
            pltpu.VMEM((share, LANES), f32),
            pltpu.VMEM((share, total_tokens), f32),
            pltpu.SemaphoreType.DMA((total_tokens // CHUNK,)),
            pltpu.SemaphoreType.DMA,
        ],
        specs=[vmem, vmem, hbm, hbm],
        elements=elements,
        flops=4 * elements * depth,
    )(code_potential, all_potential, in_hbm(codebook), in_hbm(all_tokens))
    return (targets, updated_codebook)


def solution(mesh):
    tok_size, code_size = mesh.devices.shape
    split = jax.sharding.Mesh(
        mesh.devices.reshape(tok_size, code_size // 2, 2), ("tok",) + CODE
    )
    return jax.shard_map(
        per_device,
        mesh=split,
        in_specs=(P("tok", None), P(CODE, None)),
        out_specs=(P("tok", CODE), P(CODE + ("tok",), None)),
        check_vma=False,
    )
```

```python
import functools
import math

import jax
import jax.numpy as jnp
from jax import lax
from jax.experimental import pallas as pl
from jax.experimental.pallas import tpu as pltpu
from jax.sharding import PartitionSpec as P

ITERS = 3


sharpness_factor = 2.5
rms_epsilon = 1e-06

LANES = 128
CHUNK = 1024
DOT_CHUNK = 512
AHEAD = 2
MIB = 1 << 20

score_scale = sharpness_factor * math.log2(math.e)


def lse2(values, axis):
    top = jnp.max(values, axis=axis, keepdims=True)
    total = jnp.sum(jnp.exp2(values - top), axis=axis)
    return jnp.squeeze(top, axis) + jnp.log2(total)


def as_column(row):
    return jnp.broadcast_to(row, (LANES, LANES)).T


def tile(k):
    return pl.ds(pl.multiple_of(k * LANES, LANES), LANES)


def column_lse(scores, potential, k):
    values = scores[:, tile(k)]
    if potential is not None:
        values = values + potential[...]
    values = values.reshape(values.shape[0] // 8, 8, LANES)
    top = jnp.max(values, axis=0)
    total = jnp.sum(jnp.exp2(values - top[None]), axis=0)
    most = jnp.max(top, axis=0, keepdims=True)
    total = jnp.sum(total * jnp.exp2(top - most), axis=0, keepdims=True)
    return most + jnp.log2(total)


def send_copies(local, out):
    for d in range(out.shape[0]):
        out[d] = local[...]


def chunk_copies(source, held, sems, axis=0):
    copies = []
    for k in range(source.shape[axis] // CHUNK):
        part = (slice(None),) * axis + (pl.ds(k * CHUNK, CHUNK),)
        copies.append(pltpu.make_async_copy(source.at[part], held.at[part], sems.at[k]))
    return copies


def scores_kernel(tokens, codebook, scores, out, held, rows, local, sems, rows_sem):
    copies = chunk_copies(codebook, held, sems)
    rows_copy = pltpu.make_async_copy(tokens, rows, rows_sem)
    rows_copy.start()
    for copy in copies[:AHEAD]:
        copy.start()
    rows_copy.wait()
    for k in range(len(copies) + 1):
        if k < len(copies):
            copies[k].wait()
            if k + AHEAD < len(copies):
                copies[k + AHEAD].start()
            scores[:, pl.ds(k * CHUNK, CHUNK)] = (
                lax.dot_general(
                    rows[...],
                    held[pl.ds(k * CHUNK, CHUNK), :],
                    (((1,), (1,)), ((), ())),
                    preferred_element_type=jnp.float32,
                )
                * score_scale
            )
        if k > 0:
            for j in range((k - 1) * CHUNK // LANES, k * CHUNK // LANES):
                local[pl.ds(j, 1), :] = column_lse(scores, None, j)
    send_copies(local, out)


def columns_kernel(shift, received, scores, out, column, local):
    potential = -shift - lse2(received[...], 0)
    for h in range(potential.shape[0]):
        column[pl.ds(h * LANES, LANES), :] = as_column(potential[h : h + 1, :])

    def step(k, carry):
        local[pl.ds(k, 1), :] = column_lse(scores, column, k)
        return carry

    lax.fori_loop(0, local.shape[0], step, 0, unroll=8)
    send_copies(local, out)


def rows_kernel(shift, received, scores, out, potential):
    potential[...] = -shift - lse2(received[...], 0)
    tiles = potential.shape[0]
    partials = []
    for h in range(out.shape[1]):
        rows = pl.ds(h * LANES, LANES)

        def values(k):
            return scores[rows, tile(k)] + potential[pl.ds(k, 1), :]

        top = lax.fori_loop(
            0, tiles, lambda k, top: jnp.maximum(top, values(k)), values(0), unroll=8
        )
        total = lax.fori_loop(
            0,
            tiles,
            lambda k, total: total + jnp.exp2(values(k) - top),
            jnp.zeros((LANES, LANES), jnp.float32),
            unroll=8,
        )
        partials.append((top, total))
    for h, (top, total) in enumerate(partials):
        top = top.T
        most = jnp.max(top, axis=0, keepdims=True)
        total = jnp.sum(total.T * jnp.exp2(top - most), axis=0, keepdims=True)
        local = most + jnp.log2(total)
        for d in range(out.shape[0]):
            out[d, pl.ds(h, 1), :] = local


def token_potential_kernel(shift, received, out):
    potential = -shift - lse2(received[...], 0)
    for d in range(out.shape[0]):
        out[d] = potential


def targets_kernel(
    scale, token_potential, code_potential, scores, out, column, panel, held, sems, out_sems
):
    copies = chunk_copies(scores, panel, sems, 1)
    for copy in copies:
        copy.start()
    for h in range(token_potential.shape[1]):
        column[pl.ds(h * LANES, LANES), :] = as_column(token_potential[0, pl.ds(h, 1), :]) + scale
    out_copies = chunk_copies(held, out, out_sems, 1)
    for k in range(len(copies)):
        copies[k].wait()
        for j in range(k * CHUNK // LANES, (k + 1) * CHUNK // LANES):
            held[:, tile(j)] = jnp.exp2(
                panel[:, tile(j)] + column[...] + code_potential[pl.ds(j, 1), :]
            ).astype(held.dtype)
        out_copies[k].start()
    for copy in out_copies:
        copy.wait()


def own_code_copy(codebook, codes, sem):
    share = codes.shape[0]
    start = pl.multiple_of(lax.axis_index("tok") * share, share)
    return pltpu.make_async_copy(codebook.at[pl.ds(start, share)], codes, sem)


def refresh_kernel(
    scale, code_potential, potential, codebook, tokens,
    out, held, codes, column, panel, sems, own_sem,
):
    own = own_code_copy(codebook, codes, own_sem)
    copies = chunk_copies(tokens, held, sems)
    own.start()
    for copy in copies[:AHEAD]:
        copy.start()
    halves, tiles = potential.shape[1], codes.shape[0] // LANES
    for h in range(tiles):
        row = code_potential[pl.ds(lax.axis_index("tok") * tiles + h, 1), :]
        column[pl.ds(h * LANES, LANES), :] = as_column(row) + scale
    own.wait()

    def chunk_scores(k):
        copies[k].wait()
        if k + AHEAD < len(copies):
            copies[k + AHEAD].start()
        part = pl.ds(k * CHUNK, CHUNK)
        panel[:, part] = (
            lax.dot_general(
                codes[...],
                held[part, :],
                (((1,), (1,)), ((), ())),
                preferred_element_type=jnp.float32,
            )
            * score_scale
        )

    assigned = jnp.zeros(out.shape, jnp.float32)
    chunk_scores(0)
    for k in range(len(copies)):
        if k + 1 < len(copies):
            chunk_scores(k + 1)
        for start in range(k * CHUNK, (k + 1) * CHUNK, DOT_CHUNK):
            weights = []
            for j in range(start // LANES, (start + DOT_CHUNK) // LANES):
                row = potential[j // halves, pl.ds(j % halves, 1), :]
                weights.append(
                    jnp.exp2(panel[:, tile(j)] + column[...] + row).astype(held.dtype)
                )
            assigned += jnp.dot(
                jnp.concatenate(weights, axis=1),
                held[pl.ds(start, DOT_CHUNK), :],
                preferred_element_type=jnp.float32,
            )
    mixed = codes[...].astype(jnp.float32) + assigned
    out[...] = mixed * lax.rsqrt(
        jnp.mean(mixed * mixed, axis=1, keepdims=True) + rms_epsilon
    )


def in_vmem(array):
    return pltpu.with_memory_space_constraint(array, pltpu.VMEM)


def in_hbm(array):
    return pltpu.with_memory_space_constraint(array, pltpu.HBM)


def call(kernel, out_shape, scratch=(), specs=None, out_specs=None, limit=24, elements=0, flops=0):
    vmem = pl.BlockSpec(memory_space=pltpu.VMEM)
    return pl.pallas_call(
        kernel,
        out_shape=out_shape,
        in_specs=specs,
        out_specs=out_specs if out_specs is not None else jax.tree.map(lambda _: vmem, out_shape),
        scratch_shapes=list(scratch),
        compiler_params=pltpu.CompilerParams(vmem_limit_bytes=limit * MIB),
        cost_estimate=pl.CostEstimate(
            flops=flops + 4 * elements, transcendentals=elements, bytes_accessed=4 * elements
        ),
    )


def per_device(tokens, codebook):
    tok_size, code_size = lax.axis_size("tok"), lax.axis_size("code")
    tok_rows, depth = tokens.shape
    code_rows = codebook.shape[0]
    total_tokens = tok_rows * tok_size
    total_codes = code_rows * code_size
    share = code_rows // tok_size
    row_tiles, code_tiles = tok_rows // LANES, code_rows // LANES
    elements = tok_rows * code_rows
    f32 = jnp.float32
    vmem = pl.BlockSpec(memory_space=pltpu.VMEM)
    hbm = pl.BlockSpec(memory_space=pltpu.HBM)
    to_tok = jax.ShapeDtypeStruct((tok_size, code_tiles, LANES), f32)
    to_code = jax.ShapeDtypeStruct((code_size, row_tiles, LANES), f32)
    column = pltpu.VMEM((tok_rows, LANES), f32)

    def exchange(copies, axis):
        return lax.all_to_all(copies, axis, 0, 0)

    all_tokens = lax.all_gather(tokens, "tok", axis=0, tiled=True)

    scores, copies = call(
        scores_kernel,
        (pltpu.VMEM((tok_rows, code_rows), f32), to_tok),
        [
            pltpu.VMEM((code_rows, depth), codebook.dtype),
            pltpu.VMEM((tok_rows, depth), tokens.dtype),
            pltpu.VMEM((code_tiles, LANES), f32),
            pltpu.SemaphoreType.DMA((code_rows // CHUNK,)),
            pltpu.SemaphoreType.DMA,
        ],
        specs=[hbm, hbm],
        elements=elements,
        flops=2 * elements * depth,
    )(in_hbm(tokens), in_hbm(codebook))
    for step in range(ITERS):
        last = step == ITERS - 1
        potential = pltpu.VMEM((code_tiles, LANES), f32)
        copies, *code_potential = call(
            functools.partial(rows_kernel, math.log2(total_codes)),
            (to_code, potential) if last else (to_code,),
            [] if last else [potential],
            specs=[vmem, vmem],
            elements=elements,
        )(exchange(copies, "tok"), in_vmem(scores))
        received = exchange(copies, "code")
        if not last:
            copies = call(
                functools.partial(columns_kernel, math.log2(total_tokens)),
                to_tok,
                [column, potential],
                specs=[vmem, vmem],
                elements=elements,
            )(received, in_vmem(scores))
    (code_potential,) = code_potential

    copies = call(
        functools.partial(token_potential_kernel, math.log2(total_tokens)),
        jax.ShapeDtypeStruct((tok_size, row_tiles, LANES), f32),
        specs=[vmem],
    )(received)
    all_potential = exchange(copies, "tok")
    code_sems = pltpu.SemaphoreType.DMA((code_rows // CHUNK,))
    targets = call(
        functools.partial(targets_kernel, math.log2(total_tokens)),
        jax.ShapeDtypeStruct((tok_rows, code_rows), jnp.bfloat16),
        [
            column,
            pltpu.VMEM((tok_rows, code_rows), f32),
            pltpu.VMEM((tok_rows, code_rows), jnp.bfloat16),
            code_sems,
            code_sems,
        ],
        specs=[vmem, vmem, hbm],
        out_specs=hbm,
        elements=elements,
    )(copies, code_potential, in_hbm(scores))
    updated_codebook = call(
        functools.partial(refresh_kernel, math.log2(total_tokens)),
        jax.ShapeDtypeStruct((share, depth), f32),
        [
            pltpu.VMEM((total_tokens, depth), tokens.dtype),
            pltpu.VMEM((share, depth), codebook.dtype),
            pltpu.VMEM((share, LANES), f32),
            pltpu.VMEM((share, total_tokens), f32),
            pltpu.SemaphoreType.DMA((total_tokens // CHUNK,)),
            pltpu.SemaphoreType.DMA,
        ],
        specs=[vmem, vmem, hbm, hbm],
        elements=elements,
        flops=4 * elements * depth,
    )(code_potential, all_potential, in_hbm(codebook), in_hbm(all_tokens))
    return (targets, updated_codebook)


def solution(mesh):
    return jax.shard_map(
        per_device,
        mesh=mesh,
        in_specs=(P("tok", None), P("code", None)),
        out_specs=(P("tok", "code"), P(("code", "tok"), None)),
        check_vma=False,
    )
```

```python
import functools
import math

import jax
import jax.numpy as jnp
from jax import lax
from jax.experimental import pallas as pl
from jax.experimental.pallas import tpu as pltpu
from jax.sharding import PartitionSpec as P

ITERS = 3


sharpness_factor = 2.5
rms_epsilon = 1e-06

LANES = 128
CHUNK = 1024
DOT_CHUNK = 512
AHEAD = 2
CODE = ("za", "zb", "core")
MIB = 1 << 20

score_scale = sharpness_factor * math.log2(math.e)


def lse2(values, axis):
    top = jnp.max(values, axis=axis, keepdims=True)
    total = jnp.sum(jnp.exp2(values - top), axis=axis)
    return jnp.squeeze(top, axis) + jnp.log2(total)


def as_column(row):
    return jnp.broadcast_to(row, (LANES, LANES)).T


def tile(k):
    return pl.ds(pl.multiple_of(k * LANES, LANES), LANES)


def column_lse(scores, potential, k):
    values = scores[:, tile(k)]
    if potential is not None:
        values = values + potential[...]
    values = values.reshape(values.shape[0] // 8, 8, LANES)
    top = jnp.max(values, axis=0)
    total = jnp.sum(jnp.exp2(values - top[None]), axis=0)
    most = jnp.max(top, axis=0, keepdims=True)
    total = jnp.sum(total * jnp.exp2(top - most), axis=0, keepdims=True)
    return most + jnp.log2(total)


def send_copies(local, out):
    for d in range(out.shape[0]):
        out[d] = local[...]


def chunk_copies(source, held, sems, axis=0):
    copies = []
    for k in range(source.shape[axis] // CHUNK):
        part = (slice(None),) * axis + (pl.ds(k * CHUNK, CHUNK),)
        copies.append(pltpu.make_async_copy(source.at[part], held.at[part], sems.at[k]))
    return copies


def scores_kernel(tokens, codebook, scores, out, held, rows, local, sems, rows_sem):
    copies = chunk_copies(codebook, held, sems)
    rows_copy = pltpu.make_async_copy(tokens, rows, rows_sem)
    rows_copy.start()
    for copy in copies[:AHEAD]:
        copy.start()
    rows_copy.wait()
    for k in range(len(copies) + 1):
        if k < len(copies):
            copies[k].wait()
            if k + AHEAD < len(copies):
                copies[k + AHEAD].start()
            scores[:, pl.ds(k * CHUNK, CHUNK)] = (
                lax.dot_general(
                    rows[...],
                    held[pl.ds(k * CHUNK, CHUNK), :],
                    (((1,), (1,)), ((), ())),
                    preferred_element_type=jnp.float32,
                )
                * score_scale
            )
        if k > 0:
            for j in range((k - 1) * CHUNK // LANES, k * CHUNK // LANES):
                local[pl.ds(j, 1), :] = column_lse(scores, None, j)
    send_copies(local, out)


def columns_kernel(shift, received, scores, out, column, local):
    potential = -shift - lse2(received[...], 0)
    for h in range(potential.shape[0]):
        column[pl.ds(h * LANES, LANES), :] = as_column(potential[h : h + 1, :])

    def step(k, carry):
        local[pl.ds(k, 1), :] = column_lse(scores, column, k)
        return carry

    lax.fori_loop(0, local.shape[0], step, 0, unroll=8)
    send_copies(local, out)


def rows_kernel(shift, received, scores, out, potential):
    potential[...] = -shift - lse2(received[...], 0)
    tiles = potential.shape[0]
    partials = []
    for h in range(out.shape[1]):
        rows = pl.ds(h * LANES, LANES)

        def values(k):
            return scores[rows, tile(k)] + potential[pl.ds(k, 1), :]

        top = lax.fori_loop(
            0, tiles, lambda k, top: jnp.maximum(top, values(k)), values(0), unroll=8
        )
        total = lax.fori_loop(
            0,
            tiles,
            lambda k, total: total + jnp.exp2(values(k) - top),
            jnp.zeros((LANES, LANES), jnp.float32),
            unroll=8,
        )
        partials.append((top, total))
    for h, (top, total) in enumerate(partials):
        top = top.T
        most = jnp.max(top, axis=0, keepdims=True)
        total = jnp.sum(total.T * jnp.exp2(top - most), axis=0, keepdims=True)
        local = most + jnp.log2(total)
        for d in range(out.shape[0]):
            out[d, pl.ds(h, 1), :] = local


def token_potential_kernel(shift, received, out):
    potential = -shift - lse2(received[...], 0)
    for d in range(out.shape[0]):
        out[d] = potential


def targets_kernel(
    scale, token_potential, code_potential, scores, out, column, panel, held, sems, out_sems
):
    copies = chunk_copies(scores, panel, sems, 1)
    for copy in copies:
        copy.start()
    for h in range(token_potential.shape[1]):
        column[pl.ds(h * LANES, LANES), :] = as_column(token_potential[0, pl.ds(h, 1), :]) + scale
    out_copies = chunk_copies(held, out, out_sems, 1)
    for k in range(len(copies)):
        copies[k].wait()
        for j in range(k * CHUNK // LANES, (k + 1) * CHUNK // LANES):
            held[:, tile(j)] = jnp.exp2(
                panel[:, tile(j)] + column[...] + code_potential[pl.ds(j, 1), :]
            ).astype(held.dtype)
        out_copies[k].start()
    for copy in out_copies:
        copy.wait()


def own_code_copy(codebook, codes, sem):
    share = codes.shape[0]
    start = pl.multiple_of(lax.axis_index("tok") * share, share)
    return pltpu.make_async_copy(codebook.at[pl.ds(start, share)], codes, sem)


def refresh_kernel(
    scale, code_potential, potential, codebook, tokens,
    out, held, codes, column, panel, sems, own_sem,
):
    own = own_code_copy(codebook, codes, own_sem)
    copies = chunk_copies(tokens, held, sems)
    own.start()
    for copy in copies[:AHEAD]:
        copy.start()
    halves, tiles = potential.shape[1], codes.shape[0] // LANES
    for h in range(tiles):
        row = code_potential[pl.ds(lax.axis_index("tok") * tiles + h, 1), :]
        column[pl.ds(h * LANES, LANES), :] = as_column(row) + scale
    own.wait()

    def chunk_scores(k):
        copies[k].wait()
        if k + AHEAD < len(copies):
            copies[k + AHEAD].start()
        part = pl.ds(k * CHUNK, CHUNK)
        panel[:, part] = (
            lax.dot_general(
                codes[...],
                held[part, :],
                (((1,), (1,)), ((), ())),
                preferred_element_type=jnp.float32,
            )
            * score_scale
        )

    assigned = jnp.zeros(out.shape, jnp.float32)
    chunk_scores(0)
    for k in range(len(copies)):
        if k + 1 < len(copies):
            chunk_scores(k + 1)
        for start in range(k * CHUNK, (k + 1) * CHUNK, DOT_CHUNK):
            weights = []
            for j in range(start // LANES, (start + DOT_CHUNK) // LANES):
                row = potential[j // halves, pl.ds(j % halves, 1), :]
                weights.append(
                    jnp.exp2(panel[:, tile(j)] + column[...] + row).astype(held.dtype)
                )
            assigned += jnp.dot(
                jnp.concatenate(weights, axis=1),
                held[pl.ds(start, DOT_CHUNK), :],
                preferred_element_type=jnp.float32,
            )
    mixed = codes[...].astype(jnp.float32) + assigned
    out[...] = mixed * lax.rsqrt(
        jnp.mean(mixed * mixed, axis=1, keepdims=True) + rms_epsilon
    )


def in_vmem(array):
    return pltpu.with_memory_space_constraint(array, pltpu.VMEM)


def in_hbm(array):
    return pltpu.with_memory_space_constraint(array, pltpu.HBM)


def call(kernel, out_shape, scratch=(), specs=None, out_specs=None, limit=24, elements=0, flops=0):
    vmem = pl.BlockSpec(memory_space=pltpu.VMEM)
    return pl.pallas_call(
        kernel,
        out_shape=out_shape,
        in_specs=specs,
        out_specs=out_specs if out_specs is not None else jax.tree.map(lambda _: vmem, out_shape),
        scratch_shapes=list(scratch),
        compiler_params=pltpu.CompilerParams(vmem_limit_bytes=limit * MIB),
        cost_estimate=pl.CostEstimate(
            flops=flops + 4 * elements, transcendentals=elements, bytes_accessed=4 * elements
        ),
    )


def per_device(tokens, codebook):
    tok_size, code_size = lax.axis_size("tok"), lax.axis_size(CODE)
    tok_rows, depth = tokens.shape
    code_rows = codebook.shape[0]
    total_tokens = tok_rows * tok_size
    total_codes = code_rows * code_size
    share = code_rows // tok_size
    row_tiles, code_tiles = tok_rows // LANES, code_rows // LANES
    elements = tok_rows * code_rows
    f32 = jnp.float32
    vmem = pl.BlockSpec(memory_space=pltpu.VMEM)
    hbm = pl.BlockSpec(memory_space=pltpu.HBM)
    to_tok = jax.ShapeDtypeStruct((tok_size, code_tiles, LANES), f32)
    to_code = jax.ShapeDtypeStruct((code_size, row_tiles, LANES), f32)
    column = pltpu.VMEM((tok_rows, LANES), f32)

    def exchange(copies, axis):
        return lax.all_to_all(copies, axis, 0, 0)

    sharing = ('za', 'core')
    parts = lax.axis_size(sharing)
    part_rows = tok_rows // parts
    own_part = lax.dynamic_slice_in_dim(
        tokens, lax.axis_index(sharing) * part_rows, part_rows, 0
    )
    all_tokens = lax.all_gather(own_part, ("tok",) + sharing, axis=0, tiled=True)

    scores, copies = call(
        scores_kernel,
        (pltpu.VMEM((tok_rows, code_rows), f32), to_tok),
        [
            pltpu.VMEM((code_rows, depth), codebook.dtype),
            pltpu.VMEM((tok_rows, depth), tokens.dtype),
            pltpu.VMEM((code_tiles, LANES), f32),
            pltpu.SemaphoreType.DMA((code_rows // CHUNK,)),
            pltpu.SemaphoreType.DMA,
        ],
        specs=[hbm, hbm],
        elements=elements,
        flops=2 * elements * depth,
    )(in_hbm(tokens), in_hbm(codebook))
    for step in range(ITERS):
        last = step == ITERS - 1
        potential = pltpu.VMEM((code_tiles, LANES), f32)
        copies, *code_potential = call(
            functools.partial(rows_kernel, math.log2(total_codes)),
            (to_code, potential) if last else (to_code,),
            [] if last else [potential],
            specs=[vmem, vmem],
            elements=elements,
        )(exchange(copies, "tok"), in_vmem(scores))
        received = exchange(copies, CODE)
        if not last:
            copies = call(
                functools.partial(columns_kernel, math.log2(total_tokens)),
                to_tok,
                [column, potential],
                specs=[vmem, vmem],
                elements=elements,
            )(received, in_vmem(scores))
    (code_potential,) = code_potential

    copies = call(
        functools.partial(token_potential_kernel, math.log2(total_tokens)),
        jax.ShapeDtypeStruct((tok_size, row_tiles, LANES), f32),
        specs=[vmem],
    )(received)
    all_potential = exchange(copies, "tok")
    code_sems = pltpu.SemaphoreType.DMA((code_rows // CHUNK,))
    targets = call(
        functools.partial(targets_kernel, math.log2(total_tokens)),
        jax.ShapeDtypeStruct((tok_rows, code_rows), jnp.bfloat16),
        [
            column,
            pltpu.VMEM((tok_rows, code_rows), f32),
            pltpu.VMEM((tok_rows, code_rows), jnp.bfloat16),
            code_sems,
            code_sems,
        ],
        specs=[vmem, vmem, hbm],
        out_specs=hbm,
        elements=elements,
    )(copies, code_potential, in_hbm(scores))
    updated_codebook = call(
        functools.partial(refresh_kernel, math.log2(total_tokens)),
        jax.ShapeDtypeStruct((share, depth), f32),
        [
            pltpu.VMEM((total_tokens, depth), tokens.dtype),
            pltpu.VMEM((share, depth), codebook.dtype),
            pltpu.VMEM((share, LANES), f32),
            pltpu.VMEM((share, total_tokens), f32),
            pltpu.SemaphoreType.DMA((total_tokens // CHUNK,)),
            pltpu.SemaphoreType.DMA,
        ],
        specs=[vmem, vmem, hbm, hbm],
        elements=elements,
        flops=4 * elements * depth,
    )(code_potential, all_potential, in_hbm(codebook), in_hbm(all_tokens))
    return (targets, updated_codebook)


def solution(mesh):
    tok_size, code_size = mesh.devices.shape
    split = jax.sharding.Mesh(
        mesh.devices.reshape(tok_size, code_size // 4, 2, 2), ("tok",) + CODE
    )
    return jax.shard_map(
        per_device,
        mesh=split,
        in_specs=(P("tok", None), P(CODE, None)),
        out_specs=(P("tok", CODE), P(CODE + ("tok",), None)),
        check_vma=False,
    )
```

```python
import functools
import math

import jax
import jax.numpy as jnp
from jax import lax
from jax.experimental import pallas as pl
from jax.experimental.pallas import tpu as pltpu
from jax.sharding import PartitionSpec as P

ITERS = 3


sharpness_factor = 2.5
rms_epsilon = 1e-06

LANES = 128
CHUNK = 1024
DOT_CHUNK = 512
AHEAD = 2
CODE = ("za", "zb", "core")
MIB = 1 << 20

score_scale = sharpness_factor * math.log2(math.e)


def lse2(values, axis):
    top = jnp.max(values, axis=axis, keepdims=True)
    total = jnp.sum(jnp.exp2(values - top), axis=axis)
    return jnp.squeeze(top, axis) + jnp.log2(total)


def as_column(row):
    return jnp.broadcast_to(row, (LANES, LANES)).T


def tile(k):
    return pl.ds(pl.multiple_of(k * LANES, LANES), LANES)


def column_lse(scores, potential, k):
    values = scores[:, tile(k)]
    if potential is not None:
        values = values + potential[...]
    values = values.reshape(values.shape[0] // 8, 8, LANES)
    top = jnp.max(values, axis=0)
    total = jnp.sum(jnp.exp2(values - top[None]), axis=0)
    most = jnp.max(top, axis=0, keepdims=True)
    total = jnp.sum(total * jnp.exp2(top - most), axis=0, keepdims=True)
    return most + jnp.log2(total)


def send_copies(local, out):
    for d in range(out.shape[0]):
        out[d] = local[...]


def chunk_copies(source, held, sems, axis=0):
    copies = []
    for k in range(source.shape[axis] // CHUNK):
        part = (slice(None),) * axis + (pl.ds(k * CHUNK, CHUNK),)
        copies.append(pltpu.make_async_copy(source.at[part], held.at[part], sems.at[k]))
    return copies


def scores_kernel(tokens, codebook, scores, out, held, rows, local, sems, rows_sem):
    copies = chunk_copies(codebook, held, sems)
    rows_copy = pltpu.make_async_copy(tokens, rows, rows_sem)
    rows_copy.start()
    for copy in copies[:AHEAD]:
        copy.start()
    rows_copy.wait()
    for k in range(len(copies) + 1):
        if k < len(copies):
            copies[k].wait()
            if k + AHEAD < len(copies):
                copies[k + AHEAD].start()
            scores[:, pl.ds(k * CHUNK, CHUNK)] = (
                lax.dot_general(
                    rows[...],
                    held[pl.ds(k * CHUNK, CHUNK), :],
                    (((1,), (1,)), ((), ())),
                    preferred_element_type=jnp.float32,
                )
                * score_scale
            )
        if k > 0:
            for j in range((k - 1) * CHUNK // LANES, k * CHUNK // LANES):
                local[pl.ds(j, 1), :] = column_lse(scores, None, j)
    send_copies(local, out)


def columns_kernel(shift, received, scores, out, column, local):
    potential = -shift - lse2(received[...], 0)
    for h in range(potential.shape[0]):
        column[pl.ds(h * LANES, LANES), :] = as_column(potential[h : h + 1, :])

    def step(k, carry):
        local[pl.ds(k, 1), :] = column_lse(scores, column, k)
        return carry

    lax.fori_loop(0, local.shape[0], step, 0, unroll=8)
    send_copies(local, out)


def rows_kernel(shift, received, scores, out, potential):
    potential[...] = -shift - lse2(received[...], 0)
    tiles = potential.shape[0]
    partials = []
    for h in range(out.shape[1]):
        rows = pl.ds(h * LANES, LANES)

        def values(k):
            return scores[rows, tile(k)] + potential[pl.ds(k, 1), :]

        top = lax.fori_loop(
            0, tiles, lambda k, top: jnp.maximum(top, values(k)), values(0), unroll=8
        )
        total = lax.fori_loop(
            0,
            tiles,
            lambda k, total: total + jnp.exp2(values(k) - top),
            jnp.zeros((LANES, LANES), jnp.float32),
            unroll=8,
        )
        partials.append((top, total))
    for h, (top, total) in enumerate(partials):
        top = top.T
        most = jnp.max(top, axis=0, keepdims=True)
        total = jnp.sum(total.T * jnp.exp2(top - most), axis=0, keepdims=True)
        local = most + jnp.log2(total)
        for d in range(out.shape[0]):
            out[d, pl.ds(h, 1), :] = local


def token_potential_kernel(shift, received, out):
    potential = -shift - lse2(received[...], 0)
    for d in range(out.shape[0]):
        out[d] = potential


def targets_kernel(
    scale, token_potential, code_potential, scores, out, column, panel, held, sems, out_sems
):
    copies = chunk_copies(scores, panel, sems, 1)
    for copy in copies:
        copy.start()
    for h in range(token_potential.shape[1]):
        column[pl.ds(h * LANES, LANES), :] = as_column(token_potential[0, pl.ds(h, 1), :]) + scale
    out_copies = chunk_copies(held, out, out_sems, 1)
    for k in range(len(copies)):
        copies[k].wait()
        for j in range(k * CHUNK // LANES, (k + 1) * CHUNK // LANES):
            held[:, tile(j)] = jnp.exp2(
                panel[:, tile(j)] + column[...] + code_potential[pl.ds(j, 1), :]
            ).astype(held.dtype)
        out_copies[k].start()
    for copy in out_copies:
        copy.wait()


def part_kernel(sharing, tokens, out, sem):
    rows = out.shape[0]
    start = pl.multiple_of(lax.axis_index(sharing) * rows, rows)
    copy = pltpu.make_async_copy(tokens.at[pl.ds(start, rows)], out, sem)
    copy.start()
    copy.wait()


def own_code_copy(codebook, codes, sem):
    share = codes.shape[0]
    start = pl.multiple_of(lax.axis_index("tok") * share, share)
    return pltpu.make_async_copy(codebook.at[pl.ds(start, share)], codes, sem)


def refresh_kernel(
    scale, code_potential, potential, codebook, tokens,
    out, held, codes, column, panel, sems, own_sem,
):
    own = own_code_copy(codebook, codes, own_sem)
    copies = chunk_copies(tokens, held, sems)
    own.start()
    for copy in copies[:AHEAD]:
        copy.start()
    halves, tiles = potential.shape[1], codes.shape[0] // LANES
    for h in range(tiles):
        row = code_potential[pl.ds(lax.axis_index("tok") * tiles + h, 1), :]
        column[pl.ds(h * LANES, LANES), :] = as_column(row) + scale
    own.wait()

    def chunk_scores(k):
        copies[k].wait()
        if k + AHEAD < len(copies):
            copies[k + AHEAD].start()
        part = pl.ds(k * CHUNK, CHUNK)
        panel[:, part] = (
            lax.dot_general(
                codes[...],
                held[part, :],
                (((1,), (1,)), ((), ())),
                preferred_element_type=jnp.float32,
            )
            * score_scale
        )

    assigned = jnp.zeros(out.shape, jnp.float32)
    chunk_scores(0)
    for k in range(len(copies)):
        if k + 1 < len(copies):
            chunk_scores(k + 1)
        for start in range(k * CHUNK, (k + 1) * CHUNK, DOT_CHUNK):
            weights = []
            for j in range(start // LANES, (start + DOT_CHUNK) // LANES):
                row = potential[j // halves, pl.ds(j % halves, 1), :]
                weights.append(
                    jnp.exp2(panel[:, tile(j)] + column[...] + row).astype(held.dtype)
                )
            assigned += jnp.dot(
                jnp.concatenate(weights, axis=1),
                held[pl.ds(start, DOT_CHUNK), :],
                preferred_element_type=jnp.float32,
            )
    mixed = codes[...].astype(jnp.float32) + assigned
    out[...] = mixed * lax.rsqrt(
        jnp.mean(mixed * mixed, axis=1, keepdims=True) + rms_epsilon
    )


def in_vmem(array):
    return pltpu.with_memory_space_constraint(array, pltpu.VMEM)


def in_hbm(array):
    return pltpu.with_memory_space_constraint(array, pltpu.HBM)


def call(kernel, out_shape, scratch=(), specs=None, out_specs=None, limit=24, elements=0, flops=0):
    vmem = pl.BlockSpec(memory_space=pltpu.VMEM)
    return pl.pallas_call(
        kernel,
        out_shape=out_shape,
        in_specs=specs,
        out_specs=out_specs if out_specs is not None else jax.tree.map(lambda _: vmem, out_shape),
        scratch_shapes=list(scratch),
        compiler_params=pltpu.CompilerParams(vmem_limit_bytes=limit * MIB),
        cost_estimate=pl.CostEstimate(
            flops=flops + 4 * elements, transcendentals=elements, bytes_accessed=4 * elements
        ),
    )


def per_device(tokens, codebook):
    tok_size, code_size = lax.axis_size("tok"), lax.axis_size(CODE)
    tok_rows, depth = tokens.shape
    code_rows = codebook.shape[0]
    total_tokens = tok_rows * tok_size
    total_codes = code_rows * code_size
    share = code_rows // tok_size
    row_tiles, code_tiles = tok_rows // LANES, code_rows // LANES
    elements = tok_rows * code_rows
    f32 = jnp.float32
    vmem = pl.BlockSpec(memory_space=pltpu.VMEM)
    hbm = pl.BlockSpec(memory_space=pltpu.HBM)
    to_tok = jax.ShapeDtypeStruct((tok_size, code_tiles, LANES), f32)
    to_code = jax.ShapeDtypeStruct((code_size, row_tiles, LANES), f32)
    column = pltpu.VMEM((tok_rows, LANES), f32)

    def exchange(copies, axis):
        return lax.all_to_all(copies, axis, 0, 0)

    sharing = ('za', 'core')
    parts = lax.axis_size(sharing)
    part_rows = tok_rows // parts
    own_part = call(
        functools.partial(part_kernel, sharing),
        pltpu.HBM((part_rows, depth), tokens.dtype),
        [pltpu.SemaphoreType.DMA],
        specs=[hbm],
        out_specs=hbm,
    )(in_hbm(tokens))
    all_tokens = lax.all_gather(own_part, ("tok",) + sharing, axis=0, tiled=True)

    scores, copies = call(
        scores_kernel,
        (pltpu.VMEM((tok_rows, code_rows), f32), to_tok),
        [
            pltpu.VMEM((code_rows, depth), codebook.dtype),
            pltpu.VMEM((tok_rows, depth), tokens.dtype),
            pltpu.VMEM((code_tiles, LANES), f32),
            pltpu.SemaphoreType.DMA((code_rows // CHUNK,)),
            pltpu.SemaphoreType.DMA,
        ],
        specs=[hbm, hbm],
        elements=elements,
        flops=2 * elements * depth,
    )(in_hbm(tokens), in_hbm(codebook))
    for step in range(ITERS):
        last = step == ITERS - 1
        potential = pltpu.VMEM((code_tiles, LANES), f32)
        copies, *code_potential = call(
            functools.partial(rows_kernel, math.log2(total_codes)),
            (to_code, potential) if last else (to_code,),
            [] if last else [potential],
            specs=[vmem, vmem],
            elements=elements,
        )(exchange(copies, "tok"), in_vmem(scores))
        received = exchange(copies, CODE)
        if not last:
            copies = call(
                functools.partial(columns_kernel, math.log2(total_tokens)),
                to_tok,
                [column, potential],
                specs=[vmem, vmem],
                elements=elements,
            )(received, in_vmem(scores))
    (code_potential,) = code_potential

    copies = call(
        functools.partial(token_potential_kernel, math.log2(total_tokens)),
        jax.ShapeDtypeStruct((tok_size, row_tiles, LANES), f32),
        specs=[vmem],
    )(received)
    all_potential = exchange(copies, "tok")
    code_sems = pltpu.SemaphoreType.DMA((code_rows // CHUNK,))
    targets = call(
        functools.partial(targets_kernel, math.log2(total_tokens)),
        jax.ShapeDtypeStruct((tok_rows, code_rows), jnp.bfloat16),
        [
            column,
            pltpu.VMEM((tok_rows, code_rows), f32),
            pltpu.VMEM((tok_rows, code_rows), jnp.bfloat16),
            code_sems,
            code_sems,
        ],
        specs=[vmem, vmem, hbm],
        out_specs=hbm,
        elements=elements,
    )(copies, code_potential, in_hbm(scores))
    updated_codebook = call(
        functools.partial(refresh_kernel, math.log2(total_tokens)),
        jax.ShapeDtypeStruct((share, depth), f32),
        [
            pltpu.VMEM((total_tokens, depth), tokens.dtype),
            pltpu.VMEM((share, depth), codebook.dtype),
            pltpu.VMEM((share, LANES), f32),
            pltpu.VMEM((share, total_tokens), f32),
            pltpu.SemaphoreType.DMA((total_tokens // CHUNK,)),
            pltpu.SemaphoreType.DMA,
        ],
        specs=[vmem, vmem, hbm, hbm],
        elements=elements,
        flops=4 * elements * depth,
    )(code_potential, all_potential, in_hbm(codebook), in_hbm(all_tokens))
    return (targets, updated_codebook)


def solution(mesh):
    tok_size, code_size = mesh.devices.shape
    split = jax.sharding.Mesh(
        mesh.devices.reshape(tok_size, code_size // 4, 2, 2), ("tok",) + CODE
    )
    return jax.shard_map(
        per_device,
        mesh=split,
        in_specs=(P("tok", None), P(CODE, None)),
        out_specs=(P("tok", CODE), P(CODE + ("tok",), None)),
        check_vma=False,
    )
```
